32 devices in a mesh: wide: 16 (over z, y, x), narrow: 2 (over core).
Axes of the slice: x: 2, y: 2, z: 4, core: 2. Of those that a mesh axis runs over, the one named last changes fastest.
Arguments:
- chi_in: float32 [2560, 128], P('wide', 'narrow'), may hold values from -6 to 6
- val_orb: float32 [2560, 4096], P(('wide', 'narrow')), may hold values from -4 to 4
- cond_orb: float32 [2560, 4096], P(('wide', 'narrow')), may hold values from -4 to 4
- e_val: float32 [4096], replicated, may hold values from -12 to -0.5
- e_cond: float32 [4096], replicated, may hold values from 0.5 to 12
- pair_val: int32 [1, 512], replicated, may hold values from 0 to 4095
- pair_cond: int32 [1, 512], replicated, may hold values from 0 to 4095
Outputs:
- chi_out: float32 [2560, 128], P('wide', 'narrow')
The draws below stay inside these ranges and needn't reach their ends.
All inputs are finite; a program needn't handle non-finite values.
Results may differ from the reference program's by a relative error of at most 0.0001.
Values sent between devices are 32-bit elements; how exact they have to be, the bound alone decides.
No kernel may reach another device: no remote copies, remote signals or barrier semaphores. Data moves between devices by JAX's collectives and lax.ppermute only.
A program may use at most 64 MiB of HBM per device.

```python
import jax
import jax.numpy as jnp
from jax import lax

NV = 4096
NC = 4096
PAIRS = 512
GROUPS = 1
G_DEV = 160
NG = 2560
SLAB = 128
RSUB = 4
N_WIDE = 16


def plant(drawn, key, smallest, high):
    shape = drawn.shape
    spot = [jax.random.randint(jax.random.fold_in(key, axis), (), 0, shape[axis]) for axis in range(len(shape))]
    drawn = drawn.at[tuple(spot)].set(smallest)
    longest = shape.index(max(shape))
    spot[longest] = (spot[longest] + 1) % shape[longest]
    return drawn.at[tuple(spot)].set(high)


def shard_levels(stream_key, extent, split, low, largest):
    def one(position, shards_of):
        draws = jax.random.uniform(jax.random.fold_in(jax.random.fold_in(stream_key, 6), position), (shards_of,), jnp.float32, low / len(split), largest / len(split))
        return jnp.repeat(jnp.exp(draws), extent[position] // shards_of).reshape((-1,) + (1,) * (len(extent) - position - 1))

    loudness = one(*split[0])
    for cut in split[1:]:
        loudness = loudness * one(*cut)
    return loudness


def noise(stream_key, dims, spread, most, cuts=(), kind=jnp.bfloat16):
    gain = shard_levels(stream_key, dims, cuts, -0.22, 0.18) if cuts else 1.0
    values = jax.random.normal(stream_key, dims, jnp.float32) * spread * gain
    return jnp.minimum(jnp.maximum(values, -most), most).astype(kind)


def setup_inputs(seed: int = 0) -> dict:
    arg_keys = jax.random.split(jax.random.key(seed), 8)
    chi_in = noise(arg_keys[0], (NG, SLAB), 1.0, 6.0, ((0, 16), (1, 2)), jnp.float32)
    val_orb = noise(arg_keys[1], (NG, NV), 0.6, 4.0, ((0, 32),), jnp.float32)
    cond_orb = noise(arg_keys[2], (NG, NC), 0.6, 4.0, ((0, 32),), jnp.float32)
    e_val = jnp.clip(jax.random.uniform(arg_keys[3], (NV,), jnp.float32, -12.0, -0.5), -12.0, -0.5)
    e_cond = jnp.clip(jax.random.uniform(arg_keys[4], (NC,), jnp.float32, 0.5, 12.0), 0.5, 12.0)
    pair_val = plant(jax.random.randint(arg_keys[5], (GROUPS, PAIRS), 0, NV), jax.random.fold_in(arg_keys[5], 1), 0, NV - 1).astype(jnp.int32)
    pair_cond = plant(jax.random.randint(arg_keys[6], (GROUPS, PAIRS), 0, NC), jax.random.fold_in(arg_keys[6], 1), 0, NC - 1).astype(jnp.int32)
    return {"chi_in": chi_in, "val_orb": val_orb, "cond_orb": cond_orb, "e_val": e_val, "e_cond": e_cond, "pair_val": pair_val, "pair_cond": pair_cond}


def slab_points():
    rows = jnp.arange(SLAB, dtype=jnp.int32)
    per_tile = RSUB * N_WIDE
    tile = rows // per_tile
    block = (rows // RSUB) % N_WIDE
    inner = rows % RSUB
    return (block * G_DEV + tile * RSUB + inner).astype(jnp.int32)


def reference(chi_in, val_orb, cond_orb, e_val, e_cond, pair_val, pair_cond):
    points = slab_points()
    chi = chi_in
    for block in range(GROUPS):
        dens = val_orb[:, pair_val[block]] * cond_orb[:, pair_cond[block]]
        weight = 1.0 / (e_cond[pair_cond[block]] - e_val[pair_val[block]])
        rows_part = dens[points]
        weighted = dens * weight[None, :]
        chi = chi + jnp.dot(weighted, rows_part.T, precision=lax.Precision.HIGHEST, preferred_element_type=jnp.float32)
    return chi
```

```python
import functools

import jax
import jax.numpy as jnp
from jax import lax
from jax.experimental import pallas as pl
from jax.experimental.pallas import tpu as pltpu
from jax.sharding import PartitionSpec as P

SLAB_DEV = 8
ROWS = 8
LANES = 128
CHUNK = 256
MIB = 1 << 20


def params(mib):
    return pltpu.CompilerParams(vmem_limit_bytes=mib * MIB)


def split(x, terms):
    out = []
    for _ in range(terms - 1):
        out.append(x.astype(jnp.bfloat16))
        x = x - out[-1].astype(jnp.float32)
    return out + [x.astype(jnp.bfloat16)]


def one_hot(idx, chunk):
    place = lax.broadcasted_iota(jnp.int32, (chunk, idx.shape[1]), 0)
    return jnp.where(place == (idx & (chunk - 1)), 1.0, 0.0).astype(jnp.bfloat16)


def by_chunk(rows, chunk):
    return jnp.concatenate([rows[:, at : at + chunk] for at in range(0, rows.shape[1], chunk)], axis=0)


def own_chunk(every, idx, chunk, r):
    chunk_of = idx >> (chunk.bit_length() - 1)
    out = every[:r]
    for c in range(1, every.shape[0] // r):
        out = jnp.where(chunk_of == c, every[c * r : (c + 1) * r], out)
    return out


def pick_few(rows, hot, idx):
    terms = split(by_chunk(rows, CHUNK), 3)
    m = terms[0].shape[0]
    every = jnp.dot(jnp.concatenate(terms, axis=0), hot, preferred_element_type=jnp.float32)
    return own_chunk(every[:m] + (every[m : 2 * m] + every[2 * m :]), idx, CHUNK, rows.shape[0])


def pick_many(rows, idx):
    hot = one_hot(idx, 2 * CHUNK)
    terms = jnp.concatenate(split(by_chunk(rows, 2 * CHUNK), 2), axis=1)
    every = jnp.dot(terms, jnp.concatenate([hot, hot], axis=0), preferred_element_type=jnp.float32)
    return own_chunk(every, idx, 2 * CHUNK, rows.shape[0])


def slab_kernel(val_ref, cond_ref, pv_ref, pc_ref, *refs):
    *out_refs, val, cond, pv, pc, sems = refs
    moves = ((pv_ref, pv), (pc_ref, pc), (val_ref.at[pl.ds(0, ROWS)], val), (cond_ref.at[pl.ds(0, ROWS)], cond))
    copies = [pltpu.make_async_copy(src, dst, sems.at[i]) for i, (src, dst) in enumerate(moves)]
    for copy in copies:
        copy.start()
    copies[0].wait()
    pv = pv[...]
    hot_v = one_hot(pv, CHUNK)
    copies[1].wait()
    pc = pc[...]
    hot_c = one_hot(pc, CHUNK)
    copies[2].wait()
    dens = pick_few(val[...], hot_v, pv)
    copies[3].wait()
    dens = dens * pick_few(cond[...], hot_c, pc)
    n_narrow = len(out_refs)
    sub, share = SLAB_DEV // n_narrow, dens.shape[1] // n_narrow
    for n, out_ref in enumerate(out_refs):
        for to in range(n_narrow):
            rows = dens[to * sub : (to + 1) * sub, n * share : (n + 1) * share]
            out_ref[to] = by_chunk(rows, LANES)


def with_energy(orb_ref, e_ref):
    return jnp.concatenate([orb_ref[...], jnp.broadcast_to(e_ref[...], (ROWS, e_ref.shape[1]))], axis=0)


def val_kernel(val_ref, ev_ref, pv_ref, out_ref):
    out_ref[...] = pick_many(with_energy(val_ref, ev_ref), pv_ref[...])


def dens_kernel(cond_ref, ec_ref, pc_ref, v_ref, out_ref):
    r = out_ref.shape[0]
    c = pick_many(with_energy(cond_ref, ec_ref), pc_ref[...])
    weight = 1.0 / (c[r : r + 1] - v_ref[r : r + 1])
    out_ref[...] = v_ref[:r] * c[:r] * weight


def by_source(parts, me):
    step = 1
    while step < len(parts):
        odd = (me & step) != 0
        parts = [jnp.where(odd, parts[j ^ step], parts[j]) for j in range(len(parts))]
        step *= 2
    return parts


def product_kernel(chi_ref, slab_ref, *refs):
    cols_refs, out_ref = refs[:-1], refs[-1]
    n_narrow = len(cols_refs)
    sub = SLAB_DEV // n_narrow
    contract = (((1,), (1,)), ((), ()))
    dot = functools.partial(lax.dot_general, dimension_numbers=contract, preferred_element_type=jnp.float32)
    lanes = []
    for n in range(n_narrow):
        for at in range(0, slab_ref.shape[1], sub):
            lanes.append([slab_ref[w, at : at + sub] for w in range(n, slab_ref.shape[0], n_narrow)])
    slab = jnp.concatenate([jnp.concatenate(rows, axis=0) for rows in lanes], axis=1)
    s_hi, s_lo = split(slab, 2)
    cols = by_source([ref[...] for ref in cols_refs], lax.axis_index("narrow"))
    d_hi, d_lo = split(jnp.concatenate(cols, axis=0), 2)
    out_ref[...] = chi_ref[...] + (dot(s_hi, d_hi) + (dot(s_hi, d_lo) + dot(s_lo, d_hi)))


def in_hbm(x):
    return pltpu.with_memory_space_constraint(x, pltpu.HBM)


def shards(chi_in, val_orb, cond_orb, e_val, e_cond, pair_val, pair_cond):
    n_wide, n_narrow = lax.axis_size("wide"), lax.axis_size("narrow")
    row_sub = SLAB_DEV // n_narrow
    pairs, rows, bands = pair_val.shape[1], val_orb.shape[0], val_orb.shape[1]
    tile_rows = row_sub * (pairs // n_narrow // LANES)
    vmem = pl.BlockSpec(memory_space=pltpu.VMEM)
    hbm = pl.BlockSpec(memory_space=pltpu.HBM)
    mine = pl.pallas_call(
        slab_kernel,
        in_specs=[hbm] * 4,
        out_specs=[vmem] * n_narrow,
        out_shape=[jax.ShapeDtypeStruct((n_narrow, tile_rows, LANES), jnp.float32)] * n_narrow,
        scratch_shapes=[
            pltpu.VMEM((ROWS, bands), jnp.float32),
            pltpu.VMEM((ROWS, bands), jnp.float32),
            pltpu.VMEM((1, pairs), jnp.int32),
            pltpu.VMEM((1, pairs), jnp.int32),
            pltpu.SemaphoreType.DMA((4,)),
        ],
        compiler_params=params(16),
        name="slab_rows",
    )(*(in_hbm(x) for x in (val_orb, cond_orb, pair_val, pair_cond)))
    def exchange(x, axis, bit):
        return lax.ppermute(x, axis, [(i, i ^ bit) for i in range(lax.axis_size(axis))])

    def exchange(x, bit):
        return lax.ppermute(x, "narrow", [(i, i ^ bit) for i in range(n_narrow)])

    share = mine[0]
    for n in range(1, n_narrow):
        share = jnp.where(lax.axis_index("narrow") == n, exchange(mine[n], n), share)
    parts = jnp.broadcast_to(share[None], (n_wide, *share.shape)).reshape(-1, *share.shape[1:])
    pair_val, pair_cond, parts = lax.optimization_barrier((pair_val, pair_cond, parts))
    slab = lax.all_to_all(parts, ("wide", "narrow"), 0, 0, tiled=True)
    v = pl.pallas_call(
        val_kernel,
        in_specs=[vmem] * 3,
        out_specs=vmem,
        out_shape=jax.ShapeDtypeStruct((rows + ROWS, pairs), jnp.float32),
        compiler_params=params(24),
        name="val_columns",
    )(val_orb, e_val[None, :], pair_val)
    own = pl.pallas_call(
        dens_kernel,
        in_specs=[vmem] * 4,
        out_specs=vmem,
        out_shape=jax.ShapeDtypeStruct((rows, pairs), jnp.float32),
        compiler_params=params(24),
        name="densities",
    )(cond_orb, e_cond[None, :], pair_cond, v)
    columns = [own] + [exchange(own, n) for n in range(1, n_narrow)]
    out = pl.pallas_call(
        product_kernel,
        in_specs=[vmem] * (2 + len(columns)),
        out_specs=vmem,
        out_shape=jax.ShapeDtypeStruct(chi_in.shape[::-1], jnp.float32),
        compiler_params=params(16),
        name="product",
    )(chi_in.T, slab, *columns)
    return out.T


def solution(mesh):
    placed = (
        P("wide", "narrow"),
        P(("wide", "narrow"), None),
        P(("wide", "narrow"), None),
        P(),
        P(),
        P(),
        P(),
    )
    return jax.shard_map(
        shards, mesh=mesh, in_specs=placed, out_specs=P("wide", "narrow"), check_vma=False
    )
```

```python
import functools

import jax
import jax.numpy as jnp
from jax import lax
from jax.experimental import pallas as pl
from jax.experimental.pallas import tpu as pltpu
from jax.sharding import PartitionSpec as P

SLAB_DEV = 8
ROWS = 8
LANES = 128
CHUNK = 256
MIB = 1 << 20


def params(mib):
    return pltpu.CompilerParams(vmem_limit_bytes=mib * MIB)


def split(x, terms):
    out = []
    for _ in range(terms - 1):
        out.append(x.astype(jnp.bfloat16))
        x = x - out[-1].astype(jnp.float32)
    return out + [x.astype(jnp.bfloat16)]


def one_hot(idx, chunk):
    place = lax.broadcasted_iota(jnp.int32, (chunk, idx.shape[1]), 0)
    return jnp.where(place == (idx & (chunk - 1)), 1.0, 0.0).astype(jnp.bfloat16)


def by_chunk(rows, chunk):
    return jnp.concatenate([rows[:, at : at + chunk] for at in range(0, rows.shape[1], chunk)], axis=0)


def own_chunk(every, idx, chunk, r):
    chunk_of = idx >> (chunk.bit_length() - 1)
    out = every[:r]
    for c in range(1, every.shape[0] // r):
        out = jnp.where(chunk_of == c, every[c * r : (c + 1) * r], out)
    return out


def pick_few(rows, hot, idx):
    terms = split(by_chunk(rows, CHUNK), 3)
    m = terms[0].shape[0]
    every = jnp.dot(jnp.concatenate(terms, axis=0), hot, preferred_element_type=jnp.float32)
    return own_chunk(every[:m] + (every[m : 2 * m] + every[2 * m :]), idx, CHUNK, rows.shape[0])


def pick_many(rows, idx):
    hot = one_hot(idx, 2 * CHUNK)
    terms = jnp.concatenate(split(by_chunk(rows, 2 * CHUNK), 2), axis=1)
    every = jnp.dot(terms, jnp.concatenate([hot, hot], axis=0), preferred_element_type=jnp.float32)
    return own_chunk(every, idx, 2 * CHUNK, rows.shape[0])


def slab_kernel(val_ref, cond_ref, pv_ref, pc_ref, *refs):
    *out_refs, val, cond, pv, pc, sems = refs
    moves = ((pv_ref, pv), (pc_ref, pc), (val_ref.at[pl.ds(0, ROWS)], val), (cond_ref.at[pl.ds(0, ROWS)], cond))
    copies = [pltpu.make_async_copy(src, dst, sems.at[i]) for i, (src, dst) in enumerate(moves)]
    for copy in copies:
        copy.start()
    copies[0].wait()
    pv = pv[...]
    hot_v = one_hot(pv, CHUNK)
    copies[1].wait()
    pc = pc[...]
    hot_c = one_hot(pc, CHUNK)
    copies[2].wait()
    dens = pick_few(val[...], hot_v, pv)
    copies[3].wait()
    dens = dens * pick_few(cond[...], hot_c, pc)
    n_narrow = len(out_refs)
    sub, share = SLAB_DEV // n_narrow, dens.shape[1] // n_narrow
    for n, out_ref in enumerate(out_refs):
        for to in range(n_narrow):
            out_ref[to] = by_chunk(dens[to * sub : (to + 1) * sub, n * share : (n + 1) * share], LANES)


def spread_kernel(*refs):
    *share_refs, out_ref = refs
    narrow = lax.axis_index("narrow")
    n_narrow = len(share_refs)
    share = [ref[...] for ref in share_refs]
    for n in range(1, n_narrow):
        share[0] = jnp.where(narrow == n, share[n], share[0])
    for place in range(out_ref.shape[0]):
        out_ref[place] = share[0][place % n_narrow]


def with_energy(orb_ref, e_ref):
    return jnp.concatenate([orb_ref[...], jnp.broadcast_to(e_ref[...], (ROWS, e_ref.shape[1]))], axis=0)


def val_kernel(val_ref, ev_ref, pv_ref, out_ref):
    out_ref[...] = pick_many(with_energy(val_ref, ev_ref), pv_ref[...])


def dens_kernel(cond_ref, ec_ref, pc_ref, v_ref, out_ref):
    r = out_ref.shape[0]
    c = pick_many(with_energy(cond_ref, ec_ref), pc_ref[...])
    weight = 1.0 / (c[r : r + 1] - v_ref[r : r + 1])
    out_ref[...] = v_ref[:r] * c[:r] * weight


def by_source(parts, me):
    step = 1
    while step < len(parts):
        odd = (me & step) != 0
        parts = [jnp.where(odd, parts[j ^ step], parts[j]) for j in range(len(parts))]
        step *= 2
    return parts


def columns_kernel(*refs):
    *cols_refs, hi_ref, lo_ref = refs
    cols = by_source([ref[...] for ref in cols_refs], lax.axis_index("narrow"))
    hi_ref[...], lo_ref[...] = split(jnp.concatenate(cols, axis=0).T, 2)


def product_kernel(n_narrow, chi_ref, slab_ref, hi_ref, lo_ref, out_ref):
    sub = SLAB_DEV // n_narrow
    lanes = []
    for n in range(n_narrow):
        for at in range(0, slab_ref.shape[1], sub):
            lanes.append([slab_ref[w, at : at + sub] for w in range(n, slab_ref.shape[0], n_narrow)])
    slab = jnp.concatenate([jnp.concatenate(rows, axis=0) for rows in lanes], axis=1)
    s_hi, s_lo = split(slab, 2)
    m = slab.shape[0]
    by_hi = jnp.dot(jnp.concatenate([s_hi, s_lo], axis=0), hi_ref[...], preferred_element_type=jnp.float32)
    by_lo = jnp.dot(s_hi, lo_ref[...], preferred_element_type=jnp.float32)
    out_ref[...] = chi_ref[...] + (by_hi[:m] + (by_hi[m:] + by_lo))


def in_hbm(x):
    return pltpu.with_memory_space_constraint(x, pltpu.HBM)


def shards(chi_in, val_orb, cond_orb, e_val, e_cond, pair_val, pair_cond):
    n_wide, n_narrow = lax.axis_size("wide"), lax.axis_size("narrow")
    row_sub = SLAB_DEV // n_narrow
    pairs, rows, bands = pair_val.shape[1], val_orb.shape[0], val_orb.shape[1]
    tile_rows = row_sub * (pairs // n_narrow // LANES)
    vmem = pl.BlockSpec(memory_space=pltpu.VMEM)
    hbm = pl.BlockSpec(memory_space=pltpu.HBM)
    share = jax.ShapeDtypeStruct((n_narrow, tile_rows, LANES), jnp.float32)
    mine = pl.pallas_call(
        slab_kernel,
        in_specs=[hbm] * 4,
        out_specs=[vmem] * n_narrow,
        out_shape=[share] * n_narrow,
        scratch_shapes=[
            pltpu.VMEM((ROWS, bands), jnp.float32),
            pltpu.VMEM((ROWS, bands), jnp.float32),
            pltpu.VMEM((1, pairs), jnp.int32),
            pltpu.VMEM((1, pairs), jnp.int32),
            pltpu.SemaphoreType.DMA((4,)),
        ],
        compiler_params=params(16),
        name="slab_rows",
    )(*(in_hbm(x) for x in (val_orb, cond_orb, pair_val, pair_cond)))

    def exchange(x, axis, bit):
        return lax.ppermute(x, axis, [(i, i ^ bit) for i in range(lax.axis_size(axis))])

    def exchange(x, bit):
        return lax.ppermute(x, "narrow", [(i, i ^ bit) for i in range(n_narrow)])

    parts = pl.pallas_call(
        spread_kernel,
        in_specs=[vmem] * n_narrow,
        out_specs=vmem,
        out_shape=pltpu.VMEM((n_wide * n_narrow, tile_rows, LANES), jnp.float32),
        compiler_params=params(4),
        name="spread",
    )(mine[0], *(exchange(mine[n], n) for n in range(1, n_narrow)))
    pair_val, pair_cond, parts = lax.optimization_barrier((pair_val, pair_cond, parts))
    slab = lax.all_to_all(parts, ("wide", "narrow"), 0, 0, tiled=True)
    v = pl.pallas_call(
        val_kernel,
        in_specs=[vmem] * 3,
        out_specs=vmem,
        out_shape=jax.ShapeDtypeStruct((rows + ROWS, pairs), jnp.float32),
        compiler_params=params(24),
        name="val_columns",
    )(val_orb, e_val[None, :], pair_val)
    own = pl.pallas_call(
        dens_kernel,
        in_specs=[vmem] * 4,
        out_specs=vmem,
        out_shape=jax.ShapeDtypeStruct((rows, pairs), jnp.float32),
        compiler_params=params(24),
        name="densities",
    )(cond_orb, e_cond[None, :], pair_cond, v)
    columns = [own] + [exchange(own, n) for n in range(1, n_narrow)]
    terms = pl.pallas_call(
        columns_kernel,
        in_specs=[vmem] * n_narrow,
        out_specs=[vmem] * 2,
        out_shape=[jax.ShapeDtypeStruct((pairs, n_narrow * rows), jnp.bfloat16)] * 2,
        compiler_params=params(16),
        name="columns",
    )(*columns)
    out = pl.pallas_call(
        functools.partial(product_kernel, n_narrow),
        in_specs=[vmem] * 4,
        out_specs=vmem,
        out_shape=jax.ShapeDtypeStruct(chi_in.shape[::-1], jnp.float32),
        compiler_params=params(16),
        name="product",
    )(chi_in.T, slab, *terms)
    return out.T


def solution(mesh):
    placed = (
        P("wide", "narrow"),
        P(("wide", "narrow"), None),
        P(("wide", "narrow"), None),
        P(),
        P(),
        P(),
        P(),
    )
    return jax.shard_map(
        shards, mesh=mesh, in_specs=placed, out_specs=P("wide", "narrow"), check_vma=False
    )
```

```python
import functools

import jax
import jax.numpy as jnp
from jax import lax
from jax.experimental import pallas as pl
from jax.experimental.pallas import tpu as pltpu
from jax.sharding import PartitionSpec as P

SLAB_DEV = 8
ROWS = 8
LANES = 128
CHUNK = 256
MIB = 1 << 20


def params(mib):
    return pltpu.CompilerParams(vmem_limit_bytes=mib * MIB)


def split(x, terms):
    out = []
    for _ in range(terms - 1):
        out.append(x.astype(jnp.bfloat16))
        x = x - out[-1].astype(jnp.float32)
    return out + [x.astype(jnp.bfloat16)]


def one_hot(idx, chunk):
    place = lax.broadcasted_iota(jnp.int32, (chunk, idx.shape[1]), 0)
    return jnp.where(place == (idx & (chunk - 1)), 1.0, 0.0).astype(jnp.bfloat16)


def by_chunk(rows, chunk):
    return jnp.concatenate([rows[:, at : at + chunk] for at in range(0, rows.shape[1], chunk)], axis=0)


def own_chunk(every, idx, chunk, r):
    chunk_of = idx >> (chunk.bit_length() - 1)
    out = every[:r]
    for c in range(1, every.shape[0] // r):
        out = jnp.where(chunk_of == c, every[c * r : (c + 1) * r], out)
    return out


def pick_few(rows, hot, idx):
    terms = split(by_chunk(rows, CHUNK), 3)
    m = terms[0].shape[0]
    every = jnp.dot(jnp.concatenate(terms, axis=0), hot, preferred_element_type=jnp.float32)
    return own_chunk(every[:m] + (every[m : 2 * m] + every[2 * m :]), idx, CHUNK, rows.shape[0])


def pick_many(rows, idx):
    hot = one_hot(idx, 2 * CHUNK)
    terms = jnp.concatenate(split(by_chunk(rows, 2 * CHUNK), 2), axis=1)
    every = jnp.dot(terms, jnp.concatenate([hot, hot], axis=0), preferred_element_type=jnp.float32)
    return own_chunk(every, idx, 2 * CHUNK, rows.shape[0])


def slab_kernel(val_ref, cond_ref, pv_ref, pc_ref, *refs):
    *out_refs, val, cond, pv, pc, sems = refs
    moves = ((pv_ref, pv), (pc_ref, pc), (val_ref.at[pl.ds(0, ROWS)], val), (cond_ref.at[pl.ds(0, ROWS)], cond))
    copies = [pltpu.make_async_copy(src, dst, sems.at[i]) for i, (src, dst) in enumerate(moves)]
    for copy in copies:
        copy.start()
    copies[0].wait()
    pv = pv[...]
    hot_v = one_hot(pv, CHUNK)
    copies[1].wait()
    pc = pc[...]
    hot_c = one_hot(pc, CHUNK)
    copies[2].wait()
    dens = pick_few(val[...], hot_v, pv)
    copies[3].wait()
    dens = dens * pick_few(cond[...], hot_c, pc)
    n_narrow = len(out_refs)
    sub, share = SLAB_DEV // n_narrow, dens.shape[1] // n_narrow
    for n, out_ref in enumerate(out_refs):
        for to in range(n_narrow):
            out_ref[to] = by_chunk(dens[to * sub : (to + 1) * sub, n * share : (n + 1) * share], LANES)


def spread_kernel(*refs):
    *share_refs, out_ref = refs
    narrow = lax.axis_index("narrow")
    n_narrow = len(share_refs)
    share = [ref[...] for ref in share_refs]
    for n in range(1, n_narrow):
        share[0] = jnp.where(narrow == n, share[n], share[0])
    for place in range(out_ref.shape[0]):
        out_ref[out_ref.shape[0] - 1 - place] = share[0][place % n_narrow]


def with_energy(orb_ref, e_ref):
    return jnp.concatenate([orb_ref[...], jnp.broadcast_to(e_ref[...], (ROWS, e_ref.shape[1]))], axis=0)


def val_kernel(val_ref, ev_ref, pv_ref, out_ref):
    out_ref[...] = pick_many(with_energy(val_ref, ev_ref), pv_ref[...])


def dens_kernel(cond_ref, ec_ref, pc_ref, v_ref, out_ref):
    r = out_ref.shape[0]
    c = pick_many(with_energy(cond_ref, ec_ref), pc_ref[...])
    weight = 1.0 / (c[r : r + 1] - v_ref[r : r + 1])
    out_ref[...] = v_ref[:r] * c[:r] * weight


def by_source(parts, me):
    step = 1
    while step < len(parts):
        odd = (me & step) != 0
        parts = [jnp.where(odd, parts[j ^ step], parts[j]) for j in range(len(parts))]
        step *= 2
    return parts


def columns_kernel(*refs):
    *cols_refs, hi_ref, lo_ref = refs
    cols = by_source([ref[...] for ref in cols_refs], lax.axis_index("narrow"))
    hi_ref[...], lo_ref[...] = split(jnp.concatenate(cols, axis=0).T, 2)


def product_kernel(n_narrow, chi_ref, slab_ref, hi_ref, lo_ref, out_ref):
    sub = SLAB_DEV // n_narrow
    lanes, blocks = [], slab_ref.shape[0]
    for n in range(n_narrow):
        for at in range(0, slab_ref.shape[1], sub):
            lanes.append([slab_ref[blocks - 1 - w, at : at + sub] for w in range(n, blocks, n_narrow)])
    slab = jnp.concatenate([jnp.concatenate(rows, axis=0) for rows in lanes], axis=1)
    s_hi, s_lo = split(slab, 2)
    m = slab.shape[0]
    by_hi = jnp.dot(jnp.concatenate([s_hi, s_lo], axis=0), hi_ref[...], preferred_element_type=jnp.float32)
    by_lo = jnp.dot(s_hi, lo_ref[...], preferred_element_type=jnp.float32)
    out_ref[...] = chi_ref[...] + (by_hi[:m] + (by_hi[m:] + by_lo))


def in_hbm(x):
    return pltpu.with_memory_space_constraint(x, pltpu.HBM)


def shards(chi_in, val_orb, cond_orb, e_val, e_cond, pair_val, pair_cond):
    n_wide, n_narrow = lax.axis_size("wide"), lax.axis_size("narrow")
    row_sub = SLAB_DEV // n_narrow
    pairs, rows, bands = pair_val.shape[1], val_orb.shape[0], val_orb.shape[1]
    tile_rows = row_sub * (pairs // n_narrow // LANES)
    vmem = pl.BlockSpec(memory_space=pltpu.VMEM)
    hbm = pl.BlockSpec(memory_space=pltpu.HBM)
    share = jax.ShapeDtypeStruct((n_narrow, tile_rows, LANES), jnp.float32)
    mine = pl.pallas_call(
        slab_kernel,
        in_specs=[hbm] * 4,
        out_specs=[vmem] * n_narrow,
        out_shape=[share] * n_narrow,
        scratch_shapes=[
            pltpu.VMEM((ROWS, bands), jnp.float32),
            pltpu.VMEM((ROWS, bands), jnp.float32),
            pltpu.VMEM((1, pairs), jnp.int32),
            pltpu.VMEM((1, pairs), jnp.int32),
            pltpu.SemaphoreType.DMA((4,)),
        ],
        compiler_params=params(16),
        name="slab_rows",
    )(*(in_hbm(x) for x in (val_orb, cond_orb, pair_val, pair_cond)))

    def exchange(x, axis, bit):
        return lax.ppermute(x, axis, [(i, i ^ bit) for i in range(lax.axis_size(axis))])

    def exchange(x, bit):
        return lax.ppermute(x, "narrow", [(i, i ^ bit) for i in range(n_narrow)])

    parts = pl.pallas_call(
        spread_kernel,
        in_specs=[vmem] * n_narrow,
        out_specs=vmem,
        out_shape=jax.ShapeDtypeStruct((n_wide * n_narrow, tile_rows, LANES), jnp.float32),
        compiler_params=params(16),
        name="spread",
    )(mine[0], *(exchange(mine[n], n) for n in range(1, n_narrow)))
    pair_val, pair_cond, parts = lax.optimization_barrier((pair_val, pair_cond, parts))
    last_first = [list(range(n_wide * n_narrow))[::-1]]
    slab = lax.all_to_all(parts, ("wide", "narrow"), 0, 0, axis_index_groups=last_first, tiled=True)
    v = pl.pallas_call(
        val_kernel,
        in_specs=[vmem] * 3,
        out_specs=vmem,
        out_shape=jax.ShapeDtypeStruct((rows + ROWS, pairs), jnp.float32),
        compiler_params=params(24),
        name="val_columns",
    )(val_orb, e_val[None, :], pair_val)
    own = pl.pallas_call(
        dens_kernel,
        in_specs=[vmem] * 4,
        out_specs=vmem,
        out_shape=jax.ShapeDtypeStruct((rows, pairs), jnp.float32),
        compiler_params=params(24),
        name="densities",
    )(cond_orb, e_cond[None, :], pair_cond, v)
    columns = [own] + [exchange(own, n) for n in range(1, n_narrow)]
    terms = pl.pallas_call(
        columns_kernel,
        in_specs=[vmem] * n_narrow,
        out_specs=[vmem] * 2,
        out_shape=[jax.ShapeDtypeStruct((pairs, n_narrow * rows), jnp.bfloat16)] * 2,
        compiler_params=params(16),
        name="columns",
    )(*columns)
    out = pl.pallas_call(
        functools.partial(product_kernel, n_narrow),
        in_specs=[vmem] * 4,
        out_specs=vmem,
        out_shape=jax.ShapeDtypeStruct(chi_in.shape[::-1], jnp.float32),
        compiler_params=params(16),
        name="product",
    )(chi_in.T, slab, *terms)
    return out.T


def solution(mesh):
    placed = (
        P("wide", "narrow"),
        P(("wide", "narrow"), None),
        P(("wide", "narrow"), None),
        P(),
        P(),
        P(),
        P(),
    )
    return jax.shard_map(
        shards, mesh=mesh, in_specs=placed, out_specs=P("wide", "narrow"), check_vma=False
    )
```

```python
import functools

import jax
import jax.numpy as jnp
from jax import lax
from jax.experimental import pallas as pl
from jax.experimental.pallas import tpu as pltpu
from jax.sharding import PartitionSpec as P

SLAB_DEV = 8
ROWS = 8
LANES = 128
CHUNK = 256
MIB = 1 << 20


def params(mib):
    return pltpu.CompilerParams(vmem_limit_bytes=mib * MIB)


def split(x, terms):
    out = []
    for _ in range(terms - 1):
        out.append(x.astype(jnp.bfloat16))
        x = x - out[-1].astype(jnp.float32)
    return out + [x.astype(jnp.bfloat16)]


def one_hot(idx, chunk):
    place = lax.broadcasted_iota(jnp.int32, (chunk, idx.shape[1]), 0)
    return jnp.where(place == (idx & (chunk - 1)), 1.0, 0.0).astype(jnp.bfloat16)


def by_chunk(rows, chunk):
    return jnp.concatenate([rows[:, at : at + chunk] for at in range(0, rows.shape[1], chunk)], axis=0)


def own_chunk(every, idx, chunk, r):
    chunk_of = idx >> (chunk.bit_length() - 1)
    out = every[:r]
    for c in range(1, every.shape[0] // r):
        out = jnp.where(chunk_of == c, every[c * r : (c + 1) * r], out)
    return out


def pick_few(rows, idx):
    hot = one_hot(idx, CHUNK)
    terms = split(by_chunk(rows, CHUNK), 2)
    m = terms[0].shape[0]
    every = jnp.dot(jnp.concatenate(terms, axis=0), hot, preferred_element_type=jnp.float32)
    return own_chunk(every[:m] + every[m:], idx, CHUNK, rows.shape[0])


def pick_many(rows, idx):
    hot = one_hot(idx, 2 * CHUNK)
    terms = jnp.concatenate(split(by_chunk(rows, 2 * CHUNK), 2), axis=1)
    every = jnp.dot(terms, jnp.concatenate([hot, hot], axis=0), preferred_element_type=jnp.float32)
    return own_chunk(every, idx, 2 * CHUNK, rows.shape[0])


def slab_tiles(dens, out_refs):
    n_narrow = out_refs[0].shape[0]
    sub, share = SLAB_DEV // n_narrow, dens.shape[1] // len(out_refs)
    for n, out_ref in enumerate(out_refs):
        for to in range(n_narrow):
            out_ref[to] = by_chunk(dens[to * sub : (to + 1) * sub, n * share : (n + 1) * share], LANES)


def others_kernel(val_ref, cond_ref, pv_ref, pc_ref, val, cond, pv, pc, *refs):
    *out_refs, sems = refs
    moves = ((val_ref.at[pl.ds(0, ROWS)], val), (pv_ref, pv), (cond_ref.at[pl.ds(0, ROWS)], cond), (pc_ref, pc))
    copies = [pltpu.make_async_copy(src, dst, sems.at[i]) for i, (src, dst) in enumerate(moves)]
    for copy in copies:
        copy.start()
    own = pv.shape[1] // (len(out_refs) + 1)
    copies[1].wait()
    copies[0].wait()
    dens = pick_few(val[...], pv[:, own:])
    copies[3].wait()
    copies[2].wait()
    slab_tiles(dens * pick_few(cond[...], pc[:, own:]), out_refs)


def own_kernel(val_ref, cond_ref, pv_ref, pc_ref, out_ref):
    own = pv_ref.shape[1] // out_ref.shape[0]
    dens = pick_few(val_ref[...], pv_ref[:, :own]) * pick_few(cond_ref[...], pc_ref[:, :own])
    slab_tiles(dens, [out_ref])


def spread_kernel(*refs):
    *share_refs, out_ref = refs
    narrow = lax.axis_index("narrow")
    n_narrow = len(share_refs)
    share = [ref[...] for ref in share_refs]
    for n in range(1, n_narrow):
        share[0] = jnp.where(narrow == n, share[n], share[0])
    for place in range(out_ref.shape[0]):
        out_ref[place] = share[0][place % n_narrow]


def with_energy(orb, e):
    return jnp.concatenate([orb[...], jnp.broadcast_to(e[...], (ROWS, e.shape[1]))], axis=0)


def dens_kernel(val_ref, cond_ref, ev_ref, ec_ref, pv_ref, pc_ref, out_ref, val, cond, ev, ec, pv, pc, sems):
    moves = ((val_ref, val), (ev_ref, ev), (pv_ref, pv), (cond_ref, cond), (ec_ref, ec), (pc_ref, pc))
    copies = [pltpu.make_async_copy(src, dst, sems.at[i]) for i, (src, dst) in enumerate(moves)]
    for copy in copies:
        copy.start()
    r = out_ref.shape[0]
    for copy in copies[:3]:
        copy.wait()
    v = pick_many(with_energy(val, ev), pv[...])
    for copy in copies[3:]:
        copy.wait()
    c = pick_many(with_energy(cond, ec), pc[...])
    weight = 1.0 / (c[r : r + 1] - v[r : r + 1])
    out_ref[...] = v[:r] * c[:r] * weight


def by_source(parts, me):
    step = 1
    while step < len(parts):
        odd = (me & step) != 0
        parts = [jnp.where(odd, parts[j ^ step], parts[j]) for j in range(len(parts))]
        step *= 2
    return parts


def columns_kernel(*refs):
    *cols_refs, hi_ref, lo_ref = refs
    cols = by_source([ref[...] for ref in cols_refs], lax.axis_index("narrow"))
    hi_ref[...], lo_ref[...] = split(jnp.concatenate(cols, axis=0).T, 2)


def product_kernel(n_narrow, chi_ref, slab_ref, hi_ref, lo_ref, out_ref):
    sub = SLAB_DEV // n_narrow
    lanes, blocks = [], slab_ref.shape[0]
    for n in range(n_narrow):
        for at in range(0, slab_ref.shape[1], sub):
            lanes.append([slab_ref[w, at : at + sub] for w in range(n, blocks, n_narrow)])
    slab = jnp.concatenate([jnp.concatenate(rows, axis=0) for rows in lanes], axis=1)
    s_hi, s_lo = split(slab, 2)
    m = slab.shape[0]
    by_hi = jnp.dot(jnp.concatenate([s_hi, s_lo], axis=0), hi_ref[...], preferred_element_type=jnp.float32)
    by_lo = jnp.dot(s_hi, lo_ref[...], preferred_element_type=jnp.float32)
    out_ref[...] = chi_ref[...] + (by_hi[:m] + (by_hi[m:] + by_lo))


def in_hbm(x):
    return pltpu.with_memory_space_constraint(x, pltpu.HBM)


def shards(chi_in, val_orb, cond_orb, e_val, e_cond, pair_val, pair_cond):
    n_wide, n_narrow = lax.axis_size("wide"), lax.axis_size("narrow")
    row_sub = SLAB_DEV // n_narrow
    pairs, rows, bands = pair_val.shape[1], val_orb.shape[0], val_orb.shape[1]
    tile_rows = row_sub * (pairs // n_narrow // LANES)
    vmem = pl.BlockSpec(memory_space=pltpu.VMEM)
    hbm = pl.BlockSpec(memory_space=pltpu.HBM)
    share = jax.ShapeDtypeStruct((n_narrow, tile_rows, LANES), jnp.float32)
    rows_type = jax.ShapeDtypeStruct((ROWS, bands), jnp.float32)
    pairs_type = jax.ShapeDtypeStruct((1, pairs), jnp.int32)
    first = pl.pallas_call(
        others_kernel,
        in_specs=[hbm] * 4,
        out_specs=[vmem] * (3 + n_narrow),
        out_shape=[rows_type, rows_type, pairs_type, pairs_type] + [share] * (n_narrow - 1),
        scratch_shapes=[pltpu.SemaphoreType.DMA((4,))],
        compiler_params=params(16),
        name="slab_rows_others",
    )(*(in_hbm(x) for x in (val_orb, cond_orb, pair_val, pair_cond)))
    kept, others = first[:4], first[4:]
    own_share = pl.pallas_call(
        own_kernel,
        in_specs=[vmem] * 4,
        out_specs=vmem,
        out_shape=share,
        compiler_params=params(16),
        name="slab_rows_own",
    )(*kept)

    def exchange(x, bit):
        return lax.ppermute(x, "narrow", [(i, i ^ bit) for i in range(n_narrow)])

    parts = pl.pallas_call(
        spread_kernel,
        in_specs=[vmem] * n_narrow,
        out_specs=vmem,
        out_shape=jax.ShapeDtypeStruct((n_wide * n_narrow, tile_rows, LANES), jnp.float32),
        compiler_params=params(16),
        name="spread",
    )(own_share, *(exchange(x, n) for n, x in enumerate(others, 1)))
    pair_val, pair_cond, parts = lax.optimization_barrier((pair_val, pair_cond, parts))
    slab = lax.all_to_all(parts, ("wide", "narrow"), 0, 0, tiled=True)
    operands = [val_orb, cond_orb, e_val[None, :], e_cond[None, :], pair_val, pair_cond]
    own = pl.pallas_call(
        dens_kernel,
        in_specs=[hbm] * len(operands),
        out_specs=vmem,
        out_shape=jax.ShapeDtypeStruct((rows, pairs), jnp.float32),
        scratch_shapes=[pltpu.VMEM(x.shape, x.dtype) for x in operands] + [pltpu.SemaphoreType.DMA((len(operands),))],
        compiler_params=params(32),
        name="densities",
    )(*(in_hbm(x) for x in operands))
    columns = [own] + [exchange(own, n) for n in range(1, n_narrow)]
    terms = pl.pallas_call(
        columns_kernel,
        in_specs=[vmem] * n_narrow,
        out_specs=[vmem] * 2,
        out_shape=[jax.ShapeDtypeStruct((pairs, n_narrow * rows), jnp.bfloat16)] * 2,
        compiler_params=params(16),
        name="columns",
    )(*columns)
    out = pl.pallas_call(
        functools.partial(product_kernel, n_narrow),
        in_specs=[vmem] * 4,
        out_specs=vmem,
        out_shape=jax.ShapeDtypeStruct(chi_in.shape[::-1], jnp.float32),
        compiler_params=params(16),
        name="product",
    )(chi_in.T, slab, *terms)
    return out.T


def solution(mesh):
    placed = (
        P("wide", "narrow"),
        P(("wide", "narrow"), None),
        P(("wide", "narrow"), None),
        P(),
        P(),
        P(),
        P(),
    )
    return jax.shard_map(
        shards, mesh=mesh, in_specs=placed, out_specs=P("wide", "narrow"), check_vma=False
    )
```

```python
import functools

import jax
import jax.numpy as jnp
from jax import lax
from jax.experimental import pallas as pl
from jax.experimental.pallas import tpu as pltpu
from jax.sharding import PartitionSpec as P

SLAB_DEV = 8
ROWS = 8
RADIX = 4
ORDER = (0, 2, 3, 1)
CHUNK = 256
MIB = 1 << 20


def params(mib):
    return pltpu.CompilerParams(vmem_limit_bytes=mib * MIB)


def split(x, terms):
    out = []
    for _ in range(terms - 1):
        out.append(x.astype(jnp.bfloat16))
        x = x - out[-1].astype(jnp.float32)
    return out + [x.astype(jnp.bfloat16)]


def one_hot(idx, chunk):
    place = lax.broadcasted_iota(jnp.int32, (chunk, idx.shape[1]), 0)
    return jnp.where(place == (idx & (chunk - 1)), 1.0, 0.0).astype(jnp.bfloat16)


def by_chunk(rows, chunk):
    return jnp.concatenate([rows[:, at : at + chunk] for at in range(0, rows.shape[1], chunk)], axis=0)


def own_chunk(every, idx, chunk, r):
    chunk_of = idx >> (chunk.bit_length() - 1)
    out = every[:r]
    for c in range(1, every.shape[0] // r):
        out = jnp.where(chunk_of == c, every[c * r : (c + 1) * r], out)
    return out


def pick_few(rows, idx):
    hot = one_hot(idx, CHUNK)
    terms = split(by_chunk(rows, CHUNK), 2)
    m = terms[0].shape[0]
    every = jnp.dot(jnp.concatenate(terms, axis=0), hot, preferred_element_type=jnp.float32)
    return own_chunk(every[:m] + every[m:], idx, CHUNK, rows.shape[0])


def pick_many(rows, idx):
    hot = one_hot(idx, 2 * CHUNK)
    terms = jnp.concatenate(split(by_chunk(rows, 2 * CHUNK), 2), axis=1)
    every = jnp.dot(terms, jnp.concatenate([hot, hot], axis=0), preferred_element_type=jnp.float32)
    return own_chunk(every, idx, 2 * CHUNK, rows.shape[0])


def slab_kernel(val_ref, cond_ref, pv_ref, pc_ref, out_ref, val, cond, pv, pc, sems):
    moves = ((val_ref.at[pl.ds(0, ROWS)], val), (pv_ref, pv), (cond_ref.at[pl.ds(0, ROWS)], cond), (pc_ref, pc))
    copies = [pltpu.make_async_copy(src, dst, sems.at[i]) for i, (src, dst) in enumerate(moves)]
    for copy in copies:
        copy.start()
    copies[1].wait()
    copies[0].wait()
    dens = pick_few(val[...], pv[...])
    copies[3].wait()
    copies[2].wait()
    dens = dens * pick_few(cond[...], pc[...])
    sub = out_ref.shape[1]
    for n in range(out_ref.shape[0]):
        out_ref[n] = dens[n * sub : (n + 1) * sub]


def with_energy(orb_ref, e_ref):
    return jnp.concatenate([orb_ref[...], jnp.broadcast_to(e_ref[...], (ROWS, e_ref.shape[1]))], axis=0)


def val_kernel(val_ref, ev_ref, pv_ref, out_ref):
    out_ref[...] = pick_many(with_energy(val_ref, ev_ref), pv_ref[...])


def dens_kernel(cond_ref, ec_ref, pc_ref, v_ref, out_ref):
    r = out_ref.shape[0]
    c = pick_many(with_energy(cond_ref, ec_ref), pc_ref[...])
    weight = 1.0 / (c[r : r + 1] - v_ref[r : r + 1])
    out_ref[...] = v_ref[:r] * c[:r] * weight


def by_source(parts, me):
    step = 1
    while step < len(parts):
        odd = (me & step) != 0
        parts = [jnp.where(odd, parts[j ^ step], parts[j]) for j in range(len(parts))]
        step *= 2
    return parts


def columns_kernel(*refs):
    *cols_refs, hi_ref, lo_ref = refs
    cols = by_source([ref[...] for ref in cols_refs], lax.axis_index("narrow"))
    hi_ref[...], lo_ref[...] = split(jnp.concatenate(cols, axis=0).T, 2)


def product_kernel(strides, sub, chi_ref, hi_ref, lo_ref, *refs):
    *rows_refs, out_ref = refs
    s_hi, s_lo = split(jnp.concatenate([ref[...] for ref in rows_refs], axis=0), 2)
    m = s_hi.shape[0]
    by_hi = jnp.dot(jnp.concatenate([s_hi, s_lo], axis=0), hi_ref[...], preferred_element_type=jnp.float32)
    by_lo = jnp.dot(s_hi, lo_ref[...], preferred_element_type=jnp.float32)
    total = by_hi[:m] + (by_hi[m:] + by_lo)
    blocks = m // sub
    held = {sum(s * ORDER[j // RADIX**i % RADIX] for i, s in enumerate(strides)): j for j in range(blocks)}
    parts = [total[held[x] * sub : (held[x] + 1) * sub] for x in range(blocks)]
    out_ref[...] = chi_ref[...] + jnp.concatenate(by_source(parts, lax.axis_index("wide")), axis=0)


def in_hbm(x):
    return pltpu.with_memory_space_constraint(x, pltpu.HBM)


def shards(chi_in, val_orb, cond_orb, e_val, e_cond, pair_val, pair_cond):
    n_wide, n_narrow = lax.axis_size("wide"), lax.axis_size("narrow")
    row_sub = SLAB_DEV // n_narrow
    pairs, rows, bands = pair_val.shape[1], val_orb.shape[0], val_orb.shape[1]
    vmem = pl.BlockSpec(memory_space=pltpu.VMEM)
    hbm = pl.BlockSpec(memory_space=pltpu.HBM)
    mine = pl.pallas_call(
        slab_kernel,
        in_specs=[hbm] * 4,
        out_specs=vmem,
        out_shape=jax.ShapeDtypeStruct((n_narrow, row_sub, pairs), jnp.float32),
        scratch_shapes=[
            pltpu.VMEM((ROWS, bands), jnp.float32),
            pltpu.VMEM((ROWS, bands), jnp.float32),
            pltpu.VMEM((1, pairs), jnp.int32),
            pltpu.VMEM((1, pairs), jnp.int32),
            pltpu.SemaphoreType.DMA((4,)),
        ],
        compiler_params=params(16),
        name="slab_rows",
    )(*(in_hbm(x) for x in (val_orb, cond_orb, pair_val, pair_cond)))

    def exchange(x, bit):
        return lax.ppermute(x, "narrow", [(i, i ^ bit) for i in range(n_narrow)])

    across = n_narrow - 1

    def between_chips(x, bit):
        pairs_of = [(w * n_narrow + n, (w ^ bit) * n_narrow + n ^ across) for w in range(n_wide) for n in range(n_narrow)]
        return lax.ppermute(x, ("wide", "narrow"), pairs_of)

    strides = []
    while RADIX ** (len(strides) + 1) <= n_wide:
        strides.append(n_wide // RADIX ** (len(strides) + 1))
    start = across if len(strides) % 2 else 0
    narrow = lax.axis_index("narrow")
    sent, own_block = mine[start], mine[start ^ across]
    for n in range(1, n_narrow):
        got = exchange(mine, n)
        sent = jnp.where(narrow == n, got[n ^ start], sent)
        own_block = jnp.where(narrow == n, got[n ^ start ^ across], own_block)
    pair_val, pair_cond, sent = lax.optimization_barrier((pair_val, pair_cond, sent))
    v = pl.pallas_call(
        val_kernel,
        in_specs=[vmem] * 3,
        out_specs=vmem,
        out_shape=jax.ShapeDtypeStruct((rows + ROWS, pairs), jnp.float32),
        compiler_params=params(24),
        name="val_columns",
    )(val_orb, e_val[None, :], pair_val)
    own = pl.pallas_call(
        dens_kernel,
        in_specs=[vmem] * 4,
        out_specs=vmem,
        out_shape=jax.ShapeDtypeStruct((rows, pairs), jnp.float32),
        compiler_params=params(24),
        name="densities",
    )(cond_orb, e_cond[None, :], pair_cond, v)
    got = [sent]
    for stride in strides:
        if stride == strides[0]:
            got = [own_block] + [between_chips(sent, d * stride) for d in ORDER[1:]]
            *got, own = lax.optimization_barrier((*got, own))
        else:
            sent = jnp.concatenate(got, axis=0)
            got = [exchange(sent, across)] + [between_chips(sent, d * stride) for d in ORDER[1:]]
    columns = [own] + [exchange(own, n) for n in range(1, n_narrow)]
    terms = pl.pallas_call(
        columns_kernel,
        in_specs=[vmem] * n_narrow,
        out_specs=[vmem] * 2,
        out_shape=[jax.ShapeDtypeStruct((pairs, n_narrow * rows), jnp.bfloat16)] * 2,
        compiler_params=params(16),
        name="columns",
    )(*columns)
    out = pl.pallas_call(
        functools.partial(product_kernel, tuple(strides), row_sub),
        in_specs=[vmem] * (3 + len(got)),
        out_specs=vmem,
        out_shape=jax.ShapeDtypeStruct(chi_in.shape[::-1], jnp.float32),
        compiler_params=params(16),
        name="product",
    )(chi_in.T, *terms, *got)
    return out.T


def solution(mesh):
    placed = (
        P("wide", "narrow"),
        P(("wide", "narrow"), None),
        P(("wide", "narrow"), None),
        P(),
        P(),
        P(),
        P(),
    )
    return jax.shard_map(
        shards, mesh=mesh, in_specs=placed, out_specs=P("wide", "narrow"), check_vma=False
    )
```

```python
import functools

import jax
import jax.numpy as jnp
from jax import lax
from jax.experimental import pallas as pl
from jax.experimental.pallas import tpu as pltpu
from jax.sharding import PartitionSpec as P

SLAB_DEV = 8
ROWS = 8
RADIX = 4
ORDER = (0, 2, 3, 1)
CHUNK = 256
MIB = 1 << 20


def params(mib):
    return pltpu.CompilerParams(vmem_limit_bytes=mib * MIB)


def split(x, terms):
    out = []
    for _ in range(terms - 1):
        out.append(x.astype(jnp.bfloat16))
        x = x - out[-1].astype(jnp.float32)
    return out + [x.astype(jnp.bfloat16)]


def one_hot(idx, chunk):
    place = lax.broadcasted_iota(jnp.int32, (chunk, idx.shape[1]), 0)
    return jnp.where(place == (idx & (chunk - 1)), 1.0, 0.0).astype(jnp.bfloat16)


def by_chunk(rows, chunk):
    return jnp.concatenate([rows[:, at : at + chunk] for at in range(0, rows.shape[1], chunk)], axis=0)


def own_chunk(every, idx, chunk, r):
    chunk_of = idx >> (chunk.bit_length() - 1)
    out = every[:r]
    for c in range(1, every.shape[0] // r):
        out = jnp.where(chunk_of == c, every[c * r : (c + 1) * r], out)
    return out


def pick_few(rows, idx):
    hot = one_hot(idx, CHUNK)
    terms = split(by_chunk(rows, CHUNK), 2)
    m = terms[0].shape[0]
    every = jnp.dot(jnp.concatenate(terms, axis=0), hot, preferred_element_type=jnp.float32)
    return own_chunk(every[:m] + every[m:], idx, CHUNK, rows.shape[0])


def pick_many(rows, idx):
    hot = one_hot(idx, 2 * CHUNK)
    terms = jnp.concatenate(split(by_chunk(rows, 2 * CHUNK), 2), axis=1)
    every = jnp.dot(terms, jnp.concatenate([hot, hot], axis=0), preferred_element_type=jnp.float32)
    return own_chunk(every, idx, 2 * CHUNK, rows.shape[0])


def slab_kernel(val_ref, cond_ref, pv_ref, pc_ref, out_ref, val, cond, pv, pc, sems):
    moves = ((val_ref.at[pl.ds(0, ROWS)], val), (pv_ref, pv), (cond_ref.at[pl.ds(0, ROWS)], cond), (pc_ref, pc))
    copies = [pltpu.make_async_copy(src, dst, sems.at[i]) for i, (src, dst) in enumerate(moves)]
    for copy in copies:
        copy.start()
    copies[1].wait()
    copies[0].wait()
    dens = pick_few(val[...], pv[...])
    copies[3].wait()
    copies[2].wait()
    dens = dens * pick_few(cond[...], pc[...])
    sub = out_ref.shape[1]
    for n in range(out_ref.shape[0]):
        out_ref[n] = dens[n * sub : (n + 1) * sub]


def with_energy(orb_ref, e_ref):
    return jnp.concatenate([orb_ref[...], jnp.broadcast_to(e_ref[...], (ROWS, e_ref.shape[1]))], axis=0)


def val_kernel(val_ref, ev_ref, pv_ref, out_ref):
    out_ref[...] = pick_many(with_energy(val_ref, ev_ref), pv_ref[...])


def dens_kernel(cond_ref, ec_ref, pc_ref, v_ref, out_ref):
    r = out_ref.shape[0]
    c = pick_many(with_energy(cond_ref, ec_ref), pc_ref[...])
    weight = 1.0 / (c[r : r + 1] - v_ref[r : r + 1])
    out_ref[...] = v_ref[:r] * c[:r] * weight


def by_source(parts, me):
    step = 1
    while step < len(parts):
        odd = (me & step) != 0
        parts = [jnp.where(odd, parts[j ^ step], parts[j]) for j in range(len(parts))]
        step *= 2
    return parts


def columns_kernel(*refs):
    *cols_refs, hi_ref, lo_ref = refs
    cols = by_source([ref[...] for ref in cols_refs], lax.axis_index("narrow"))
    hi_ref[...], lo_ref[...] = split(jnp.concatenate(cols, axis=0).T, 2)


def product_kernel(strides, sub, chi_ref, hi_ref, lo_ref, *refs):
    *rows_refs, out_ref = refs
    s_hi, s_lo = split(jnp.concatenate([ref[...] for ref in rows_refs], axis=0), 2)
    m = s_hi.shape[0]
    by_hi = jnp.dot(jnp.concatenate([s_hi, s_lo], axis=0), hi_ref[...], preferred_element_type=jnp.float32)
    by_lo = jnp.dot(s_hi, lo_ref[...], preferred_element_type=jnp.float32)
    total = by_hi[:m] + (by_hi[m:] + by_lo)
    blocks = m // sub
    held = {sum(s * ORDER[j // RADIX**i % RADIX] for i, s in enumerate(strides)): j for j in range(blocks)}
    parts = [total[held[x] * sub : (held[x] + 1) * sub] for x in range(blocks)]
    out_ref[...] = chi_ref[...] + jnp.concatenate(by_source(parts, lax.axis_index("wide")), axis=0)


def in_hbm(x):
    return pltpu.with_memory_space_constraint(x, pltpu.HBM)


def shards(chi_in, val_orb, cond_orb, e_val, e_cond, pair_val, pair_cond):
    n_wide, n_narrow = lax.axis_size("wide"), lax.axis_size("narrow")
    row_sub = SLAB_DEV // n_narrow
    pairs, rows, bands = pair_val.shape[1], val_orb.shape[0], val_orb.shape[1]
    vmem = pl.BlockSpec(memory_space=pltpu.VMEM)
    hbm = pl.BlockSpec(memory_space=pltpu.HBM)
    mine = pl.pallas_call(
        slab_kernel,
        in_specs=[hbm] * 4,
        out_specs=vmem,
        out_shape=jax.ShapeDtypeStruct((n_narrow, row_sub, pairs), jnp.float32),
        scratch_shapes=[
            pltpu.VMEM((ROWS, bands), jnp.float32),
            pltpu.VMEM((ROWS, bands), jnp.float32),
            pltpu.VMEM((1, pairs), jnp.int32),
            pltpu.VMEM((1, pairs), jnp.int32),
            pltpu.SemaphoreType.DMA((4,)),
        ],
        compiler_params=params(16),
        name="slab_rows",
    )(*(in_hbm(x) for x in (val_orb, cond_orb, pair_val, pair_cond)))

    def exchange(x, bit):
        return lax.ppermute(x, "narrow", [(i, i ^ bit) for i in range(n_narrow)])

    across = n_narrow - 1

    def between_chips(x, bit):
        pairs_of = [(w * n_narrow + n, (w ^ bit) * n_narrow + n ^ across) for w in range(n_wide) for n in range(n_narrow)]
        return lax.ppermute(x, ("wide", "narrow"), pairs_of)

    strides = []
    while RADIX ** (len(strides) + 1) <= n_wide:
        strides.append(n_wide // RADIX ** (len(strides) + 1))
    start = across if len(strides) % 2 else 0
    narrow = lax.axis_index("narrow")
    sent, own_block = mine[start], mine[start ^ across]
    for n in range(1, n_narrow):
        got = exchange(mine, n)
        sent = jnp.where(narrow == n, got[n ^ start], sent)
        own_block = jnp.where(narrow == n, got[n ^ start ^ across], own_block)
    pair_val, pair_cond, sent = lax.optimization_barrier((pair_val, pair_cond, sent))
    v = pl.pallas_call(
        val_kernel,
        in_specs=[vmem] * 3,
        out_specs=vmem,
        out_shape=jax.ShapeDtypeStruct((rows + ROWS, pairs), jnp.float32),
        compiler_params=params(24),
        name="val_columns",
    )(val_orb, e_val[None, :], pair_val)
    own = pl.pallas_call(
        dens_kernel,
        in_specs=[vmem] * 4,
        out_specs=vmem,
        out_shape=jax.ShapeDtypeStruct((rows, pairs), jnp.float32),
        compiler_params=params(24),
        name="densities",
    )(cond_orb, e_cond[None, :], pair_cond, v)
    columns = [own] + [exchange(own, n) for n in range(1, n_narrow)]
    got = [sent]
    for stride in strides:
        if stride == strides[0]:
            got = [own_block] + [between_chips(sent, d * stride) for d in ORDER[1:]]
            *got, own = lax.optimization_barrier((*got, own))
        else:
            sent = jnp.concatenate(got, axis=0)
            got = [between_chips(sent, d * stride) for d in ORDER[1:]]
            sent, got[0] = lax.optimization_barrier((sent, got[0]))
            got = [exchange(sent, across)] + got
    terms = pl.pallas_call(
        columns_kernel,
        in_specs=[vmem] * n_narrow,
        out_specs=[vmem] * 2,
        out_shape=[jax.ShapeDtypeStruct((pairs, n_narrow * rows), jnp.bfloat16)] * 2,
        compiler_params=params(16),
        name="columns",
    )(*columns)
    out = pl.pallas_call(
        functools.partial(product_kernel, tuple(strides), row_sub),
        in_specs=[vmem] * (3 + len(got)),
        out_specs=vmem,
        out_shape=jax.ShapeDtypeStruct(chi_in.shape[::-1], jnp.float32),
        compiler_params=params(16),
        name="product",
    )(chi_in.T, *terms, *got)
    return out.T


def solution(mesh):
    placed = (
        P("wide", "narrow"),
        P(("wide", "narrow"), None),
        P(("wide", "narrow"), None),
        P(),
        P(),
        P(),
        P(),
    )
    return jax.shard_map(
        shards, mesh=mesh, in_specs=placed, out_specs=P("wide", "narrow"), check_vma=False
    )
```

```python
import functools

import jax
import jax.numpy as jnp
from jax import lax
from jax.experimental import pallas as pl
from jax.experimental.pallas import tpu as pltpu
from jax.sharding import PartitionSpec as P

SLAB_DEV = 8
ROWS = 8
RADIX = 4
STEPS = ((2, 3, 1, 0), (3, 2, 0, 1), (1, 0, 3, 2))
CHUNK = 256
MIB = 1 << 20


def params(mib):
    return pltpu.CompilerParams(vmem_limit_bytes=mib * MIB)


def split(x, terms):
    out = []
    for _ in range(terms - 1):
        out.append(x.astype(jnp.bfloat16))
        x = x - out[-1].astype(jnp.float32)
    return out + [x.astype(jnp.bfloat16)]


def one_hot(idx, chunk):
    place = lax.broadcasted_iota(jnp.int32, (chunk, idx.shape[1]), 0)
    return jnp.where(place == (idx & (chunk - 1)), 1.0, 0.0).astype(jnp.bfloat16)


def by_chunk(rows, chunk):
    return jnp.concatenate([rows[:, at : at + chunk] for at in range(0, rows.shape[1], chunk)], axis=0)


def own_chunk(every, idx, chunk, r):
    chunk_of = idx >> (chunk.bit_length() - 1)
    out = every[:r]
    for c in range(1, every.shape[0] // r):
        out = jnp.where(chunk_of == c, every[c * r : (c + 1) * r], out)
    return out


def pick_few(rows, hot, idx):
    terms = split(by_chunk(rows, CHUNK), 2)
    m = terms[0].shape[0]
    every = jnp.dot(jnp.concatenate(terms, axis=0), hot, preferred_element_type=jnp.float32)
    return own_chunk(every[:m] + every[m:], idx, CHUNK, rows.shape[0])


def pick_many(rows, idx):
    hot = one_hot(idx, 2 * CHUNK)
    terms = jnp.concatenate(split(by_chunk(rows, 2 * CHUNK), 2), axis=1)
    every = jnp.dot(terms, jnp.concatenate([hot, hot], axis=0), preferred_element_type=jnp.float32)
    return own_chunk(every, idx, 2 * CHUNK, rows.shape[0])


def slab_kernel(val_ref, cond_ref, pv_ref, pc_ref, out_ref, val, cond, pv, pc, sems):
    moves = ((pv_ref, pv), (pc_ref, pc), (val_ref.at[pl.ds(0, ROWS)], val), (cond_ref.at[pl.ds(0, ROWS)], cond))
    copies = [pltpu.make_async_copy(src, dst, sems.at[i]) for i, (src, dst) in enumerate(moves)]
    for copy in copies:
        copy.start(priority=1)
    copies[0].wait()
    hot_v = one_hot(pv[...], CHUNK)
    copies[1].wait()
    hot_c = one_hot(pc[...], CHUNK)
    copies[2].wait()
    dens = pick_few(val[...], hot_v, pv[...])
    copies[3].wait()
    dens = dens * pick_few(cond[...], hot_c, pc[...])
    sub = out_ref.shape[1]
    for n in range(out_ref.shape[0]):
        out_ref[n] = dens[n * sub : (n + 1) * sub]


def with_energy(orb_ref, e_ref):
    return jnp.concatenate([orb_ref[...], jnp.broadcast_to(e_ref[...], (ROWS, e_ref.shape[1]))], axis=0)


def val_kernel(val_ref, ev_ref, pv_ref, out_ref):
    out_ref[...] = pick_many(with_energy(val_ref, ev_ref), pv_ref[...])


def dens_kernel(cond_ref, ec_ref, pc_ref, v_ref, out_ref):
    r = out_ref.shape[0]
    c = pick_many(with_energy(cond_ref, ec_ref), pc_ref[...])
    weight = 1.0 / (c[r : r + 1] - v_ref[r : r + 1])
    out_ref[...] = v_ref[:r] * c[:r] * weight


def by_source(parts, me):
    step = 1
    while step < len(parts):
        odd = (me & step) != 0
        parts = [jnp.where(odd, parts[j ^ step], parts[j]) for j in range(len(parts))]
        step *= 2
    return parts


def columns_kernel(*refs):
    *cols_refs, hi_ref, lo_ref = refs
    cols = by_source([ref[...] for ref in cols_refs], lax.axis_index("narrow"))
    hi_ref[...], lo_ref[...] = split(jnp.concatenate(cols, axis=0).T, 2)


def by_digit(parts, place):
    from_place = [[here] + [step.index(here) for step in STEPS] for here in range(RADIX)]
    out = []
    for source in range(RADIX):
        part = parts[from_place[0].index(source)]
        for here in range(1, RADIX):
            part = jnp.where(place == here, parts[from_place[here].index(source)], part)
        out.append(part)
    return out


def product_kernel(strides, sub, chi_ref, hi_ref, lo_ref, *refs):
    *rows_refs, out_ref = refs
    s_hi, s_lo = split(jnp.concatenate([ref[...] for ref in rows_refs], axis=0), 2)
    m = s_hi.shape[0]
    by_hi = jnp.dot(jnp.concatenate([s_hi, s_lo], axis=0), hi_ref[...], preferred_element_type=jnp.float32)
    by_lo = jnp.dot(s_hi, lo_ref[...], preferred_element_type=jnp.float32)
    total = by_hi[:m] + (by_hi[m:] + by_lo)
    wide = lax.axis_index("wide")
    parts = [total[at : at + sub] for at in range(0, m, sub)]
    for i, stride in enumerate(strides):
        place, low = lax.rem(lax.div(wide, stride), RADIX), RADIX**i
        for j in range(len(parts)):
            if j // low % RADIX == 0:
                held = [j + k * low for k in range(RADIX)]
                for at, part in zip(held, by_digit([parts[at] for at in held], place)):
                    parts[at] = part
    held = {sum(s * (j // RADIX**i % RADIX) for i, s in enumerate(strides)): j for j in range(len(parts))}
    out_ref[...] = chi_ref[...] + jnp.concatenate([parts[held[w]] for w in range(len(parts))], axis=0)


def in_hbm(x):
    return pltpu.with_memory_space_constraint(x, pltpu.HBM)


def shards(chi_in, val_orb, cond_orb, e_val, e_cond, pair_val, pair_cond):
    n_wide, n_narrow = lax.axis_size("wide"), lax.axis_size("narrow")
    row_sub = SLAB_DEV // n_narrow
    pairs, rows, bands = pair_val.shape[1], val_orb.shape[0], val_orb.shape[1]
    vmem = pl.BlockSpec(memory_space=pltpu.VMEM)
    hbm = pl.BlockSpec(memory_space=pltpu.HBM)
    mine = pl.pallas_call(
        slab_kernel,
        in_specs=[hbm] * 4,
        out_specs=vmem,
        out_shape=jax.ShapeDtypeStruct((n_narrow, row_sub, pairs), jnp.float32),
        scratch_shapes=[
            pltpu.VMEM((ROWS, bands), jnp.float32),
            pltpu.VMEM((ROWS, bands), jnp.float32),
            pltpu.VMEM((1, pairs), jnp.int32),
            pltpu.VMEM((1, pairs), jnp.int32),
            pltpu.SemaphoreType.DMA((4,)),
        ],
        compiler_params=params(16),
        name="slab_rows",
    )(*(in_hbm(x) for x in (val_orb, cond_orb, pair_val, pair_cond)))

    def exchange(x, bit):
        return lax.ppermute(x, "narrow", [(i, i ^ bit) for i in range(n_narrow)])

    across = n_narrow - 1

    def between_chips(x, step, stride):
        pairs_of = []
        for w in range(n_wide):
            place = w // stride % RADIX
            to = w + (step[place] - place) * stride
            pairs_of += [(w * n_narrow + n, to * n_narrow + (n ^ across)) for n in range(n_narrow)]
        return lax.ppermute(x, ("wide", "narrow"), pairs_of)

    strides = []
    while RADIX ** (len(strides) + 1) <= n_wide:
        strides.append(n_wide // RADIX ** (len(strides) + 1))
    start = across if len(strides) % 2 else 0
    narrow = lax.axis_index("narrow")
    sent, own_block = mine[start], mine[start ^ across]
    for n in range(1, n_narrow):
        got = exchange(mine, n)
        sent = jnp.where(narrow == n, got[n ^ start], sent)
        own_block = jnp.where(narrow == n, got[n ^ start ^ across], own_block)
    pair_val, pair_cond, sent = lax.optimization_barrier((pair_val, pair_cond, sent))
    v = pl.pallas_call(
        val_kernel,
        in_specs=[vmem] * 3,
        out_specs=vmem,
        out_shape=jax.ShapeDtypeStruct((rows + ROWS, pairs), jnp.float32),
        compiler_params=params(24),
        name="val_columns",
    )(val_orb, e_val[None, :], pair_val)
    own = pl.pallas_call(
        dens_kernel,
        in_specs=[vmem] * 4,
        out_specs=vmem,
        out_shape=jax.ShapeDtypeStruct((rows, pairs), jnp.float32),
        compiler_params=params(24),
        name="densities",
    )(cond_orb, e_cond[None, :], pair_cond, v)
    columns = [own] + [exchange(own, n) for n in range(1, n_narrow)]
    got = [sent]
    for stride in strides:
        if stride == strides[0]:
            got = [own_block] + [between_chips(sent, step, stride) for step in STEPS]
            *got, own = lax.optimization_barrier((*got, own))
        else:
            sent = jnp.concatenate(got, axis=0)
            got = [between_chips(sent, step, stride) for step in STEPS]
            sent, got[0] = lax.optimization_barrier((sent, got[0]))
            got = [exchange(sent, across)] + got
    terms = pl.pallas_call(
        columns_kernel,
        in_specs=[vmem] * n_narrow,
        out_specs=[vmem] * 2,
        out_shape=[jax.ShapeDtypeStruct((pairs, n_narrow * rows), jnp.bfloat16)] * 2,
        compiler_params=params(16),
        name="columns",
    )(*columns)
    out = pl.pallas_call(
        functools.partial(product_kernel, tuple(strides), row_sub),
        in_specs=[vmem] * (3 + len(got)),
        out_specs=vmem,
        out_shape=jax.ShapeDtypeStruct(chi_in.shape[::-1], jnp.float32),
        compiler_params=params(16),
        name="product",
    )(chi_in.T, *terms, *got)
    return out.T


def solution(mesh):
    placed = (
        P("wide", "narrow"),
        P(("wide", "narrow"), None),
        P(("wide", "narrow"), None),
        P(),
        P(),
        P(),
        P(),
    )
    return jax.shard_map(
        shards, mesh=mesh, in_specs=placed, out_specs=P("wide", "narrow"), check_vma=False
    )
```

```python
import functools

import jax
import jax.numpy as jnp
from jax import lax
from jax.experimental import pallas as pl
from jax.experimental.pallas import tpu as pltpu
from jax.sharding import PartitionSpec as P

SLAB_DEV = 8
ROWS = 8
RADIX = 4
ROUNDS = (
    ((2, 3, 1, 0), (3, 2, 0, 1), (1, 0, 3, 2)),
    ((2, 0, 3, 1), (1, 3, 0, 2), (3, 2, 1, 0)),
)
CHUNK = 256
MIB = 1 << 20


def params(mib):
    return pltpu.CompilerParams(vmem_limit_bytes=mib * MIB)


def split(x, terms):
    out = []
    for _ in range(terms - 1):
        out.append(x.astype(jnp.bfloat16))
        x = x - out[-1].astype(jnp.float32)
    return out + [x.astype(jnp.bfloat16)]


def one_hot(idx, chunk):
    place = lax.broadcasted_iota(jnp.int32, (chunk, idx.shape[1]), 0)
    return jnp.where(place == (idx & (chunk - 1)), 1.0, 0.0).astype(jnp.bfloat16)


def by_chunk(rows, chunk):
    return jnp.concatenate([rows[:, at : at + chunk] for at in range(0, rows.shape[1], chunk)], axis=0)


def own_chunk(every, idx, chunk, r):
    chunk_of = idx >> (chunk.bit_length() - 1)
    out = every[:r]
    for c in range(1, every.shape[0] // r):
        out = jnp.where(chunk_of == c, every[c * r : (c + 1) * r], out)
    return out


def pick_few(rows, hot, idx):
    terms = split(by_chunk(rows, CHUNK), 2)
    m = terms[0].shape[0]
    every = jnp.dot(jnp.concatenate(terms, axis=0), hot, preferred_element_type=jnp.float32)
    return own_chunk(every[:m] + every[m:], idx, CHUNK, rows.shape[0])


def pick_many(rows, idx):
    hot = one_hot(idx, 2 * CHUNK)
    terms = jnp.concatenate(split(by_chunk(rows, 2 * CHUNK), 2), axis=1)
    every = jnp.dot(terms, jnp.concatenate([hot, hot], axis=0), preferred_element_type=jnp.float32)
    return own_chunk(every, idx, 2 * CHUNK, rows.shape[0])


def slab_kernel(val_ref, cond_ref, pv_ref, pc_ref, out_ref, val, cond, pv, pc, sems):
    moves = ((pv_ref, pv), (pc_ref, pc), (val_ref.at[pl.ds(0, ROWS)], val), (cond_ref.at[pl.ds(0, ROWS)], cond))
    copies = [pltpu.make_async_copy(src, dst, sems.at[i]) for i, (src, dst) in enumerate(moves)]
    for copy in copies:
        copy.start(priority=1)
    copies[0].wait()
    hot_v = one_hot(pv[...], CHUNK)
    copies[1].wait()
    hot_c = one_hot(pc[...], CHUNK)
    copies[2].wait()
    dens = pick_few(val[...], hot_v, pv[...])
    copies[3].wait()
    dens = dens * pick_few(cond[...], hot_c, pc[...])
    sub = out_ref.shape[1]
    for n in range(out_ref.shape[0]):
        out_ref[n] = dens[n * sub : (n + 1) * sub]


def with_energy(orb_ref, e_ref):
    return jnp.concatenate([orb_ref[...], jnp.broadcast_to(e_ref[...], (ROWS, e_ref.shape[1]))], axis=0)


def val_kernel(val_ref, ev_ref, pv_ref, out_ref):
    out_ref[...] = pick_many(with_energy(val_ref, ev_ref), pv_ref[...])


def dens_kernel(cond_ref, ec_ref, pc_ref, v_ref, out_ref):
    r = out_ref.shape[0]
    c = pick_many(with_energy(cond_ref, ec_ref), pc_ref[...])
    weight = 1.0 / (c[r : r + 1] - v_ref[r : r + 1])
    out_ref[...] = v_ref[:r] * c[:r] * weight


def by_source(parts, me):
    step = 1
    while step < len(parts):
        odd = (me & step) != 0
        parts = [jnp.where(odd, parts[j ^ step], parts[j]) for j in range(len(parts))]
        step *= 2
    return parts


def columns_kernel(*refs):
    *cols_refs, hi_ref, lo_ref = refs
    cols = by_source([ref[...] for ref in cols_refs], lax.axis_index("narrow"))
    hi_ref[...], lo_ref[...] = split(jnp.concatenate(cols, axis=0).T, 2)


def by_digit(parts, place, steps):
    from_place = [[here] + [step.index(here) for step in steps] for here in range(RADIX)]
    out = []
    for source in range(RADIX):
        part = parts[from_place[0].index(source)]
        for here in range(1, RADIX):
            part = jnp.where(place == here, parts[from_place[here].index(source)], part)
        out.append(part)
    return out


def product_kernel(strides, sub, chi_ref, hi_ref, lo_ref, *refs):
    *rows_refs, out_ref = refs
    s_hi, s_lo = split(jnp.concatenate([ref[...] for ref in rows_refs], axis=0), 2)
    m = s_hi.shape[0]
    by_hi = jnp.dot(jnp.concatenate([s_hi, s_lo], axis=0), hi_ref[...], preferred_element_type=jnp.float32)
    by_lo = jnp.dot(s_hi, lo_ref[...], preferred_element_type=jnp.float32)
    total = by_hi[:m] + (by_hi[m:] + by_lo)
    wide = lax.axis_index("wide")
    parts = [total[at : at + sub] for at in range(0, m, sub)]
    for i, stride in enumerate(strides):
        place, low = lax.rem(lax.div(wide, stride), RADIX), RADIX**i
        for j in range(len(parts)):
            if j // low % RADIX == 0:
                held = [j + k * low for k in range(RADIX)]
                for at, part in zip(held, by_digit([parts[at] for at in held], place, ROUNDS[i % len(ROUNDS)])):
                    parts[at] = part
    held = {sum(s * (j // RADIX**i % RADIX) for i, s in enumerate(strides)): j for j in range(len(parts))}
    out_ref[...] = chi_ref[...] + jnp.concatenate([parts[held[w]] for w in range(len(parts))], axis=0)


def in_hbm(x):
    return pltpu.with_memory_space_constraint(x, pltpu.HBM)


def shards(chi_in, val_orb, cond_orb, e_val, e_cond, pair_val, pair_cond):
    n_wide, n_narrow = lax.axis_size("wide"), lax.axis_size("narrow")
    row_sub = SLAB_DEV // n_narrow
    pairs, rows, bands = pair_val.shape[1], val_orb.shape[0], val_orb.shape[1]
    vmem = pl.BlockSpec(memory_space=pltpu.VMEM)
    hbm = pl.BlockSpec(memory_space=pltpu.HBM)
    mine = pl.pallas_call(
        slab_kernel,
        in_specs=[hbm] * 4,
        out_specs=vmem,
        out_shape=jax.ShapeDtypeStruct((n_narrow, row_sub, pairs), jnp.float32),
        scratch_shapes=[
            pltpu.VMEM((ROWS, bands), jnp.float32),
            pltpu.VMEM((ROWS, bands), jnp.float32),
            pltpu.VMEM((1, pairs), jnp.int32),
            pltpu.VMEM((1, pairs), jnp.int32),
            pltpu.SemaphoreType.DMA((4,)),
        ],
        compiler_params=params(16),
        name="slab_rows",
    )(*(in_hbm(x) for x in (val_orb, cond_orb, pair_val, pair_cond)))

    def exchange(x, bit):
        return lax.ppermute(x, "narrow", [(i, i ^ bit) for i in range(n_narrow)])

    across = n_narrow - 1

    def between_chips(x, step, stride):
        pairs_of = []
        for w in range(n_wide):
            place = w // stride % RADIX
            to = w + (step[place] - place) * stride
            pairs_of += [(w * n_narrow + n, to * n_narrow + (n ^ across)) for n in range(n_narrow)]
        return lax.ppermute(x, ("wide", "narrow"), pairs_of)

    strides = []
    while RADIX ** (len(strides) + 1) <= n_wide:
        strides.append(n_wide // RADIX ** (len(strides) + 1))
    start = across if len(strides) % 2 else 0
    narrow = lax.axis_index("narrow")
    sent, own_block = mine[start], mine[start ^ across]
    for n in range(1, n_narrow):
        got = exchange(mine, n)
        sent = jnp.where(narrow == n, got[n ^ start], sent)
        own_block = jnp.where(narrow == n, got[n ^ start ^ across], own_block)
    pair_val, pair_cond, sent = lax.optimization_barrier((pair_val, pair_cond, sent))
    v = pl.pallas_call(
        val_kernel,
        in_specs=[vmem] * 3,
        out_specs=vmem,
        out_shape=jax.ShapeDtypeStruct((rows + ROWS, pairs), jnp.float32),
        compiler_params=params(24),
        name="val_columns",
    )(val_orb, e_val[None, :], pair_val)
    own = pl.pallas_call(
        dens_kernel,
        in_specs=[vmem] * 4,
        out_specs=vmem,
        out_shape=jax.ShapeDtypeStruct((rows, pairs), jnp.float32),
        compiler_params=params(24),
        name="densities",
    )(cond_orb, e_cond[None, :], pair_cond, v)
    columns = [own] + [exchange(own, n) for n in range(1, n_narrow)]
    got = [sent]
    for i, stride in enumerate(strides):
        steps = ROUNDS[i % len(ROUNDS)]
        if i == 0:
            got = [own_block] + [between_chips(sent, step, stride) for step in steps]
            *got, own = lax.optimization_barrier((*got, own))
        else:
            sent = jnp.concatenate(got, axis=0)
            got = [between_chips(sent, step, stride) for step in steps]
            sent, got[0] = lax.optimization_barrier((sent, got[0]))
            got = [exchange(sent, across)] + got
    terms = pl.pallas_call(
        columns_kernel,
        in_specs=[vmem] * n_narrow,
        out_specs=[vmem] * 2,
        out_shape=[jax.ShapeDtypeStruct((pairs, n_narrow * rows), jnp.bfloat16)] * 2,
        compiler_params=params(16),
        name="columns",
    )(*columns)
    out = pl.pallas_call(
        functools.partial(product_kernel, tuple(strides), row_sub),
        in_specs=[vmem] * (3 + len(got)),
        out_specs=vmem,
        out_shape=jax.ShapeDtypeStruct(chi_in.shape[::-1], jnp.float32),
        compiler_params=params(16),
        name="product",
    )(chi_in.T, *terms, *got)
    return out.T


def solution(mesh):
    placed = (
        P("wide", "narrow"),
        P(("wide", "narrow"), None),
        P(("wide", "narrow"), None),
        P(),
        P(),
        P(),
        P(),
    )
    return jax.shard_map(
        shards, mesh=mesh, in_specs=placed, out_specs=P("wide", "narrow"), check_vma=False
    )
```

```python
import functools

import jax
import jax.numpy as jnp
from jax import lax
from jax.experimental import pallas as pl
from jax.experimental.pallas import tpu as pltpu
from jax.sharding import PartitionSpec as P

SLAB_DEV = 8
ROWS = 8
RADIX = 4
ROUNDS = (
    ((2, 3, 1, 0), (3, 2, 0, 1), (1, 0, 3, 2)),
    ((3, 2, 1, 0), (1, 0, 3, 2), (2, 3, 0, 1)),
)
CHUNK = 256
MIB = 1 << 20


def params(mib):
    return pltpu.CompilerParams(vmem_limit_bytes=mib * MIB)


def split(x, terms):
    out = []
    for _ in range(terms - 1):
        out.append(x.astype(jnp.bfloat16))
        x = x - out[-1].astype(jnp.float32)
    return out + [x.astype(jnp.bfloat16)]


def one_hot(idx, chunk):
    place = lax.broadcasted_iota(jnp.int32, (chunk, idx.shape[1]), 0)
    return jnp.where(place == (idx & (chunk - 1)), 1.0, 0.0).astype(jnp.bfloat16)


def by_chunk(rows, chunk):
    return jnp.concatenate([rows[:, at : at + chunk] for at in range(0, rows.shape[1], chunk)], axis=0)


def own_chunk(every, idx, chunk, r):
    chunk_of = idx >> (chunk.bit_length() - 1)
    out = every[:r]
    for c in range(1, every.shape[0] // r):
        out = jnp.where(chunk_of == c, every[c * r : (c + 1) * r], out)
    return out


def pick_few(rows, hot, idx):
    terms = split(by_chunk(rows, CHUNK), 2)
    m = terms[0].shape[0]
    every = jnp.dot(jnp.concatenate(terms, axis=0), hot, preferred_element_type=jnp.float32)
    return own_chunk(every[:m] + every[m:], idx, CHUNK, rows.shape[0])


def pick_many(rows, idx):
    hot = one_hot(idx, 2 * CHUNK)
    terms = jnp.concatenate(split(by_chunk(rows, 2 * CHUNK), 2), axis=1)
    every = jnp.dot(terms, jnp.concatenate([hot, hot], axis=0), preferred_element_type=jnp.float32)
    return own_chunk(every, idx, 2 * CHUNK, rows.shape[0])


def slab_kernel(val_ref, cond_ref, pv_ref, pc_ref, out_ref, val, cond, pv, pc, sems):
    moves = ((pv_ref, pv), (pc_ref, pc), (val_ref.at[pl.ds(0, ROWS)], val), (cond_ref.at[pl.ds(0, ROWS)], cond))
    copies = [pltpu.make_async_copy(src, dst, sems.at[i]) for i, (src, dst) in enumerate(moves)]
    for copy in copies:
        copy.start(priority=1)
    copies[0].wait()
    hot_v = one_hot(pv[...], CHUNK)
    copies[1].wait()
    hot_c = one_hot(pc[...], CHUNK)
    copies[2].wait()
    dens = pick_few(val[...], hot_v, pv[...])
    copies[3].wait()
    dens = dens * pick_few(cond[...], hot_c, pc[...])
    sub = out_ref.shape[1]
    for n in range(out_ref.shape[0]):
        out_ref[n] = dens[n * sub : (n + 1) * sub]


def with_energy(orb_ref, e_ref):
    return jnp.concatenate([orb_ref[...], jnp.broadcast_to(e_ref[...], (ROWS, e_ref.shape[1]))], axis=0)


def val_kernel(val_ref, ev_ref, pv_ref, out_ref):
    out_ref[...] = pick_many(with_energy(val_ref, ev_ref), pv_ref[...])


def dens_kernel(cond_ref, ec_ref, pc_ref, v_ref, out_ref):
    r = out_ref.shape[0]
    c = pick_many(with_energy(cond_ref, ec_ref), pc_ref[...])
    weight = 1.0 / (c[r : r + 1] - v_ref[r : r + 1])
    out_ref[...] = v_ref[:r] * c[:r] * weight


def by_source(parts, me):
    step = 1
    while step < len(parts):
        odd = (me & step) != 0
        parts = [jnp.where(odd, parts[j ^ step], parts[j]) for j in range(len(parts))]
        step *= 2
    return parts


def columns_kernel(*refs):
    *cols_refs, hi_ref, lo_ref = refs
    cols = by_source([ref[...] for ref in cols_refs], lax.axis_index("narrow"))
    hi_ref[...], lo_ref[...] = split(jnp.concatenate(cols, axis=0).T, 2)


def by_digit(parts, place, steps):
    from_place = [[here] + [step.index(here) for step in steps] for here in range(RADIX)]
    out = []
    for source in range(RADIX):
        part = parts[from_place[0].index(source)]
        for here in range(1, RADIX):
            part = jnp.where(place == here, parts[from_place[here].index(source)], part)
        out.append(part)
    return out


def product_kernel(strides, sub, chi_ref, hi_ref, lo_ref, *refs):
    *rows_refs, out_ref = refs
    s_hi, s_lo = split(jnp.concatenate([ref[...] for ref in rows_refs], axis=0), 2)
    m = s_hi.shape[0]
    by_hi = jnp.dot(jnp.concatenate([s_hi, s_lo], axis=0), hi_ref[...], preferred_element_type=jnp.float32)
    by_lo = jnp.dot(s_hi, lo_ref[...], preferred_element_type=jnp.float32)
    total = by_hi[:m] + (by_hi[m:] + by_lo)
    wide = lax.axis_index("wide")
    parts = [total[at : at + sub] for at in range(0, m, sub)]
    for i, stride in enumerate(strides):
        place, low = lax.rem(lax.div(wide, stride), RADIX), RADIX**i
        for j in range(len(parts)):
            if j // low % RADIX == 0:
                held = [j + k * low for k in range(RADIX)]
                for at, part in zip(held, by_digit([parts[at] for at in held], place, ROUNDS[i % len(ROUNDS)])):
                    parts[at] = part
    held = {sum(s * (j // RADIX**i % RADIX) for i, s in enumerate(strides)): j for j in range(len(parts))}
    out_ref[...] = chi_ref[...] + jnp.concatenate([parts[held[w]] for w in range(len(parts))], axis=0)


def in_hbm(x):
    return pltpu.with_memory_space_constraint(x, pltpu.HBM)


def shards(chi_in, val_orb, cond_orb, e_val, e_cond, pair_val, pair_cond):
    n_wide, n_narrow = lax.axis_size("wide"), lax.axis_size("narrow")
    row_sub = SLAB_DEV // n_narrow
    pairs, rows, bands = pair_val.shape[1], val_orb.shape[0], val_orb.shape[1]
    vmem = pl.BlockSpec(memory_space=pltpu.VMEM)
    hbm = pl.BlockSpec(memory_space=pltpu.HBM)
    mine = pl.pallas_call(
        slab_kernel,
        in_specs=[hbm] * 4,
        out_specs=vmem,
        out_shape=jax.ShapeDtypeStruct((n_narrow, row_sub, pairs), jnp.float32),
        scratch_shapes=[
            pltpu.VMEM((ROWS, bands), jnp.float32),
            pltpu.VMEM((ROWS, bands), jnp.float32),
            pltpu.VMEM((1, pairs), jnp.int32),
            pltpu.VMEM((1, pairs), jnp.int32),
            pltpu.SemaphoreType.DMA((4,)),
        ],
        compiler_params=params(16),
        name="slab_rows",
    )(*(in_hbm(x) for x in (val_orb, cond_orb, pair_val, pair_cond)))

    def exchange(x, bit):
        return lax.ppermute(x, "narrow", [(i, i ^ bit) for i in range(n_narrow)])

    across = n_narrow - 1

    def between_chips(x, step, stride):
        pairs_of = []
        for w in range(n_wide):
            place = w // stride % RADIX
            to = w + (step[place] - place) * stride
            pairs_of += [(w * n_narrow + n, to * n_narrow + (n ^ across)) for n in range(n_narrow)]
        return lax.ppermute(x, ("wide", "narrow"), pairs_of)

    strides = []
    while RADIX ** (len(strides) + 1) <= n_wide:
        strides.append(n_wide // RADIX ** (len(strides) + 1))
    start = across if len(strides) % 2 else 0
    narrow = lax.axis_index("narrow")
    sent, own_block = mine[start], mine[start ^ across]
    for n in range(1, n_narrow):
        got = exchange(mine, n)
        sent = jnp.where(narrow == n, got[n ^ start], sent)
        own_block = jnp.where(narrow == n, got[n ^ start ^ across], own_block)
    pair_val, pair_cond, sent = lax.optimization_barrier((pair_val, pair_cond, sent))
    v = pl.pallas_call(
        val_kernel,
        in_specs=[vmem] * 3,
        out_specs=vmem,
        out_shape=jax.ShapeDtypeStruct((rows + ROWS, pairs), jnp.float32),
        compiler_params=params(24),
        name="val_columns",
    )(val_orb, e_val[None, :], pair_val)
    own = pl.pallas_call(
        dens_kernel,
        in_specs=[vmem] * 4,
        out_specs=vmem,
        out_shape=jax.ShapeDtypeStruct((rows, pairs), jnp.float32),
        compiler_params=params(24),
        name="densities",
    )(cond_orb, e_cond[None, :], pair_cond, v)
    columns = [own] + [exchange(own, n) for n in range(1, n_narrow)]
    got = [sent]
    for i, stride in enumerate(strides):
        steps = ROUNDS[i % len(ROUNDS)]
        if i == 0:
            got = [own_block] + [between_chips(sent, step, stride) for step in steps]
            *got, own = lax.optimization_barrier((*got, own))
        else:
            sent = jnp.concatenate(got, axis=0)
            got = [between_chips(sent, step, stride) for step in steps]
            sent, got[0] = lax.optimization_barrier((sent, got[0]))
            got = [exchange(sent, across)] + got
    terms = pl.pallas_call(
        columns_kernel,
        in_specs=[vmem] * n_narrow,
        out_specs=[vmem] * 2,
        out_shape=[jax.ShapeDtypeStruct((pairs, n_narrow * rows), jnp.bfloat16)] * 2,
        compiler_params=params(16),
        name="columns",
    )(*columns)
    out = pl.pallas_call(
        functools.partial(product_kernel, tuple(strides), row_sub),
        in_specs=[vmem] * (3 + len(got)),
        out_specs=vmem,
        out_shape=jax.ShapeDtypeStruct(chi_in.shape[::-1], jnp.float32),
        compiler_params=params(16),
        name="product",
    )(chi_in.T, *terms, *got)
    return out.T


def solution(mesh):
    placed = (
        P("wide", "narrow"),
        P(("wide", "narrow"), None),
        P(("wide", "narrow"), None),
        P(),
        P(),
        P(),
        P(),
    )
    return jax.shard_map(
        shards, mesh=mesh, in_specs=placed, out_specs=P("wide", "narrow"), check_vma=False
    )
```

```python
import functools

import jax
import jax.numpy as jnp
from jax import lax
from jax.experimental import pallas as pl
from jax.experimental.pallas import tpu as pltpu
from jax.sharding import PartitionSpec as P

SLAB_DEV = 8
ROWS = 8
RADIX = 4
ROUNDS = (
    ((2, 3, 1, 0), (3, 2, 0, 1), (1, 0, 3, 2)),
    ((3, 2, 1, 0), (1, 0, 3, 2), (2, 3, 0, 1)),
)
CHUNK = 256
MIB = 1 << 20


def params(mib):
    return pltpu.CompilerParams(vmem_limit_bytes=mib * MIB)


def split(x, terms):
    out = []
    for _ in range(terms - 1):
        out.append(x.astype(jnp.bfloat16))
        x = x - out[-1].astype(jnp.float32)
    return out + [x.astype(jnp.bfloat16)]


def one_hot(idx, chunk):
    place = lax.broadcasted_iota(jnp.int32, (chunk, idx.shape[1]), 0)
    return jnp.where(place == (idx & (chunk - 1)), 1.0, 0.0).astype(jnp.bfloat16)


def by_chunk(rows, chunk):
    return jnp.concatenate([rows[:, at : at + chunk] for at in range(0, rows.shape[1], chunk)], axis=0)


def own_chunk(every, idx, chunk, r):
    chunk_of = idx >> (chunk.bit_length() - 1)
    out = every[:r]
    for c in range(1, every.shape[0] // r):
        out = jnp.where(chunk_of == c, every[c * r : (c + 1) * r], out)
    return out


def pick_few(rows, hot, idx):
    terms = split(by_chunk(rows, 2 * CHUNK), 2)
    m = terms[0].shape[0]
    every = jnp.dot(jnp.concatenate(terms, axis=0), hot, preferred_element_type=jnp.float32)
    return own_chunk(every[:m] + every[m:], idx, 2 * CHUNK, rows.shape[0])


def pick_many(rows, idx):
    hot = one_hot(idx, 2 * CHUNK)
    terms = jnp.concatenate(split(by_chunk(rows, 2 * CHUNK), 2), axis=1)
    every = jnp.dot(terms, jnp.concatenate([hot, hot], axis=0), preferred_element_type=jnp.float32)
    return own_chunk(every, idx, 2 * CHUNK, rows.shape[0])


def slab_kernel(val_ref, cond_ref, pv_ref, pc_ref, out_ref, val, cond, pv, pc, sems):
    moves = ((pv_ref, pv), (pc_ref, pc), (val_ref.at[pl.ds(0, ROWS)], val), (cond_ref.at[pl.ds(0, ROWS)], cond))
    copies = [pltpu.make_async_copy(src, dst, sems.at[i]) for i, (src, dst) in enumerate(moves)]
    for copy in copies:
        copy.start(priority=1)
    copies[0].wait()
    hot_v = one_hot(pv[...], 2 * CHUNK)
    copies[1].wait()
    hot_c = one_hot(pc[...], 2 * CHUNK)
    copies[2].wait()
    dens = pick_few(val[...], hot_v, pv[...])
    copies[3].wait()
    dens = dens * pick_few(cond[...], hot_c, pc[...])
    sub = out_ref.shape[1]
    for n in range(out_ref.shape[0]):
        out_ref[n] = dens[n * sub : (n + 1) * sub]


def with_energy(orb_ref, e_ref):
    return jnp.concatenate([orb_ref[...], jnp.broadcast_to(e_ref[...], (ROWS, e_ref.shape[1]))], axis=0)


def val_kernel(val_ref, ev_ref, pv_ref, out_ref):
    out_ref[...] = pick_many(with_energy(val_ref, ev_ref), pv_ref[...])


def dens_kernel(cond_ref, ec_ref, pc_ref, v_ref, out_ref):
    r = out_ref.shape[0]
    c = pick_many(with_energy(cond_ref, ec_ref), pc_ref[...])
    weight = 1.0 / (c[r : r + 1] - v_ref[r : r + 1])
    out_ref[...] = v_ref[:r] * c[:r] * weight


def by_source(parts, me):
    step = 1
    while step < len(parts):
        odd = (me & step) != 0
        parts = [jnp.where(odd, parts[j ^ step], parts[j]) for j in range(len(parts))]
        step *= 2
    return parts


def columns_kernel(*refs):
    *cols_refs, hi_ref, lo_ref = refs
    cols = by_source([ref[...] for ref in cols_refs], lax.axis_index("narrow"))
    hi_ref[...], lo_ref[...] = split(jnp.concatenate(cols, axis=0).T, 2)


def by_digit(parts, place, steps):
    from_place = [[here] + [step.index(here) for step in steps] for here in range(RADIX)]
    out = []
    for source in range(RADIX):
        part = parts[from_place[0].index(source)]
        for here in range(1, RADIX):
            part = jnp.where(place == here, parts[from_place[here].index(source)], part)
        out.append(part)
    return out


def product_kernel(stride, steps, sub, chi_ref, hi_ref, lo_ref, *refs):
    *rows_refs, out_ref = refs
    s_hi, s_lo = split(jnp.concatenate([ref[...] for ref in rows_refs], axis=0), 2)
    m = s_hi.shape[0]
    by_hi = jnp.dot(jnp.concatenate([s_hi, s_lo], axis=0), hi_ref[...], preferred_element_type=jnp.float32)
    by_lo = jnp.dot(s_hi, lo_ref[...], preferred_element_type=jnp.float32)
    total = by_hi[:m] + (by_hi[m:] + by_lo)
    place, each = lax.rem(lax.div(lax.axis_index("wide"), stride), RADIX), m // len(rows_refs)
    parts = by_digit([total[at : at + each] for at in range(0, m, each)], place, steps)
    rows = [part[at : at + sub] for at in range(0, each, sub) for part in parts]
    out_ref[...] = chi_ref[...] + jnp.concatenate(rows, axis=0)


def in_hbm(x):
    return pltpu.with_memory_space_constraint(x, pltpu.HBM)


def shards(chi_in, val_orb, cond_orb, e_val, e_cond, pair_val, pair_cond):
    n_wide, n_narrow = lax.axis_size("wide"), lax.axis_size("narrow")
    row_sub = SLAB_DEV // n_narrow
    pairs, rows, bands = pair_val.shape[1], val_orb.shape[0], val_orb.shape[1]
    vmem = pl.BlockSpec(memory_space=pltpu.VMEM)
    hbm = pl.BlockSpec(memory_space=pltpu.HBM)
    mine = pl.pallas_call(
        slab_kernel,
        in_specs=[hbm] * 4,
        out_specs=vmem,
        out_shape=jax.ShapeDtypeStruct((n_narrow, row_sub, pairs), jnp.float32),
        scratch_shapes=[
            pltpu.VMEM((ROWS, bands), jnp.float32),
            pltpu.VMEM((ROWS, bands), jnp.float32),
            pltpu.VMEM((1, pairs), jnp.int32),
            pltpu.VMEM((1, pairs), jnp.int32),
            pltpu.SemaphoreType.DMA((4,)),
        ],
        compiler_params=params(16),
        name="slab_rows",
    )(*(in_hbm(x) for x in (val_orb, cond_orb, pair_val, pair_cond)))

    def exchange(x, bit):
        return lax.ppermute(x, "narrow", [(i, i ^ bit) for i in range(n_narrow)])

    across = n_narrow - 1

    def between_chips(x, step, stride):
        pairs_of = []
        for w in range(n_wide):
            place = w // stride % RADIX
            to = w + (step[place] - place) * stride
            pairs_of += [(w * n_narrow + n, to * n_narrow + (n ^ across)) for n in range(n_narrow)]
        return lax.ppermute(x, ("wide", "narrow"), pairs_of)

    def in_order(blocks, stride, steps):
        blocks = by_digit(blocks, lax.rem(lax.div(lax.axis_index("wide"), stride), RADIX), steps)
        groups = blocks[0].shape[0] // row_sub
        if groups == 1:
            return jnp.concatenate(blocks, axis=0)
        joined = jnp.stack([block.reshape(groups, row_sub, pairs) for block in blocks], axis=1)
        return joined.reshape(-1, pairs)

    strides = []
    while RADIX ** (len(strides) + 1) <= n_wide:
        strides.append(n_wide // RADIX ** (len(strides) + 1))
    start = across if len(strides) % 2 else 0
    narrow = lax.axis_index("narrow")
    sent, own_block = mine[start], mine[start ^ across]
    for n in range(1, n_narrow):
        got = exchange(mine, n)
        sent = jnp.where(narrow == n, got[n ^ start], sent)
        own_block = jnp.where(narrow == n, got[n ^ start ^ across], own_block)
    pair_val, pair_cond, sent = lax.optimization_barrier((pair_val, pair_cond, sent))
    v = pl.pallas_call(
        val_kernel,
        in_specs=[vmem] * 3,
        out_specs=vmem,
        out_shape=jax.ShapeDtypeStruct((rows + ROWS, pairs), jnp.float32),
        compiler_params=params(24),
        name="val_columns",
    )(val_orb, e_val[None, :], pair_val)
    own = pl.pallas_call(
        dens_kernel,
        in_specs=[vmem] * 4,
        out_specs=vmem,
        out_shape=jax.ShapeDtypeStruct((rows, pairs), jnp.float32),
        compiler_params=params(24),
        name="densities",
    )(cond_orb, e_cond[None, :], pair_cond, v)
    columns = [own] + [exchange(own, n) for n in range(1, n_narrow)]
    got = [sent]
    for i, stride in enumerate(strides):
        steps = ROUNDS[i % len(ROUNDS)]
        if i == 0:
            got = [own_block] + [between_chips(sent, step, stride) for step in steps]
            *got, own = lax.optimization_barrier((*got, own))
        else:
            sent = in_order(got, strides[i - 1], ROUNDS[(i - 1) % len(ROUNDS)])
            got = [between_chips(sent, step, stride) for step in steps]
            sent, got[0] = lax.optimization_barrier((sent, got[0]))
            got = [exchange(sent, across)] + got
    terms = pl.pallas_call(
        columns_kernel,
        in_specs=[vmem] * n_narrow,
        out_specs=[vmem] * 2,
        out_shape=[jax.ShapeDtypeStruct((pairs, n_narrow * rows), jnp.bfloat16)] * 2,
        compiler_params=params(16),
        name="columns",
    )(*columns)
    out = pl.pallas_call(
        functools.partial(product_kernel, strides[-1], ROUNDS[(len(strides) - 1) % len(ROUNDS)], row_sub),
        in_specs=[vmem] * (3 + len(got)),
        out_specs=vmem,
        out_shape=jax.ShapeDtypeStruct(chi_in.shape[::-1], jnp.float32),
        compiler_params=params(16),
        name="product",
    )(chi_in.T, *terms, *got)
    return out.T


def solution(mesh):
    placed = (
        P("wide", "narrow"),
        P(("wide", "narrow"), None),
        P(("wide", "narrow"), None),
        P(),
        P(),
        P(),
        P(),
    )
    return jax.shard_map(
        shards, mesh=mesh, in_specs=placed, out_specs=P("wide", "narrow"), check_vma=False
    )
```

```python
import functools

import jax
import jax.numpy as jnp
from jax import lax
from jax.experimental import pallas as pl
from jax.experimental.pallas import tpu as pltpu
from jax.sharding import PartitionSpec as P

SLAB_DEV = 8
ROWS = 8
RADIX = 4
ROUNDS = (
    ((2, 3, 1, 0), (3, 2, 0, 1), (1, 0, 3, 2)),
    ((3, 2, 1, 0), (1, 0, 3, 2), (2, 3, 0, 1)),
)
CHUNK = 256
MIB = 1 << 20


def params(mib):
    return pltpu.CompilerParams(vmem_limit_bytes=mib * MIB)


def split(x, terms):
    out = []
    for _ in range(terms - 1):
        out.append(x.astype(jnp.bfloat16))
        x = x - out[-1].astype(jnp.float32)
    return out + [x.astype(jnp.bfloat16)]


def one_hot(idx, chunk):
    place = lax.broadcasted_iota(jnp.int32, (chunk, idx.shape[1]), 0)
    return jnp.where(place == (idx & (chunk - 1)), 1.0, 0.0).astype(jnp.bfloat16)


def by_chunk(rows, chunk):
    return jnp.concatenate([rows[:, at : at + chunk] for at in range(0, rows.shape[1], chunk)], axis=0)


def own_chunk(every, idx, chunk, r):
    chunk_of = idx >> (chunk.bit_length() - 1)
    out = every[:r]
    for c in range(1, every.shape[0] // r):
        out = jnp.where(chunk_of == c, every[c * r : (c + 1) * r], out)
    return out


def pick_few(rows, hot, idx):
    terms = split(by_chunk(rows, CHUNK), 2)
    m = terms[0].shape[0]
    every = jnp.dot(jnp.concatenate(terms, axis=0), hot, preferred_element_type=jnp.float32)
    return own_chunk(every[:m] + every[m:], idx, CHUNK, rows.shape[0])


def pick_many(rows, idx):
    hot = one_hot(idx, 2 * CHUNK)
    terms = jnp.concatenate(split(by_chunk(rows, 2 * CHUNK), 2), axis=1)
    every = jnp.dot(terms, jnp.concatenate([hot, hot], axis=0), preferred_element_type=jnp.float32)
    return own_chunk(every, idx, 2 * CHUNK, rows.shape[0])


def slab_kernel(val_ref, cond_ref, pv_ref, pc_ref, out_ref, val, cond, pv, pc, sems):
    moves = ((pv_ref, pv), (pc_ref, pc), (val_ref.at[pl.ds(0, ROWS)], val), (cond_ref.at[pl.ds(0, ROWS)], cond))
    copies = [pltpu.make_async_copy(src, dst, sems.at[i]) for i, (src, dst) in enumerate(moves)]
    for copy in copies:
        copy.start(priority=1)
    copies[0].wait()
    hot_v = one_hot(pv[...], CHUNK)
    copies[1].wait()
    hot_c = one_hot(pc[...], CHUNK)
    copies[2].wait()
    dens = pick_few(val[...], hot_v, pv[...])
    copies[3].wait()
    dens = dens * pick_few(cond[...], hot_c, pc[...])
    sub = out_ref.shape[1]
    for n in range(out_ref.shape[0]):
        out_ref[n] = dens[n * sub : (n + 1) * sub]


def with_energy(orb_ref, e_ref):
    return jnp.concatenate([orb_ref[...], jnp.broadcast_to(e_ref[...], (ROWS, e_ref.shape[1]))], axis=0)


def val_kernel(val_ref, ev_ref, pv_ref, out_ref):
    out_ref[...] = pick_many(with_energy(val_ref, ev_ref), pv_ref[...])


def dens_kernel(cond_ref, ec_ref, pc_ref, v_ref, out_ref):
    r = out_ref.shape[0]
    c = pick_many(with_energy(cond_ref, ec_ref), pc_ref[...])
    weight = 1.0 / (c[r : r + 1] - v_ref[r : r + 1])
    out_ref[...] = v_ref[:r] * c[:r] * weight


def by_source(parts, me):
    step = 1
    while step < len(parts):
        odd = (me & step) != 0
        parts = [jnp.where(odd, parts[j ^ step], parts[j]) for j in range(len(parts))]
        step *= 2
    return parts


def columns_kernel(*refs):
    *cols_refs, hi_ref, lo_ref = refs
    cols = by_source([ref[...] for ref in cols_refs], lax.axis_index("narrow"))
    hi_ref[...], lo_ref[...] = split(jnp.concatenate(cols, axis=0).T, 2)


def by_digit(parts, place, steps):
    from_place = [[here] + [step.index(here) for step in steps] for here in range(RADIX)]
    out = []
    for source in range(RADIX):
        part = parts[from_place[0].index(source)]
        for here in range(1, RADIX):
            part = jnp.where(place == here, parts[from_place[here].index(source)], part)
        out.append(part)
    return out


def product_kernel(stride, steps, sub, chi_ref, hi_ref, lo_ref, *refs):
    *rows_refs, out_ref = refs
    s_hi, s_lo = split(jnp.concatenate([ref[...] for ref in rows_refs], axis=0), 2)
    m = s_hi.shape[0]
    by_hi = jnp.dot(jnp.concatenate([s_hi, s_lo], axis=0), hi_ref[...], preferred_element_type=jnp.float32)
    by_lo = jnp.dot(s_hi, lo_ref[...], preferred_element_type=jnp.float32)
    total = by_hi[:m] + (by_hi[m:] + by_lo)
    place, each = lax.rem(lax.div(lax.axis_index("wide"), stride), RADIX), m // len(rows_refs)
    parts = by_digit([total[at : at + each] for at in range(0, m, each)], place, steps)
    rows = [part[at : at + sub] for at in range(0, each, sub) for part in parts]
    out_ref[...] = chi_ref[...] + jnp.concatenate(rows, axis=0)


def in_hbm(x):
    return pltpu.with_memory_space_constraint(x, pltpu.HBM)


def shards(chi_in, val_orb, cond_orb, e_val, e_cond, pair_val, pair_cond):
    n_wide, n_narrow = lax.axis_size("wide"), lax.axis_size("narrow")
    row_sub = SLAB_DEV // n_narrow
    pairs, rows, bands = pair_val.shape[1], val_orb.shape[0], val_orb.shape[1]
    vmem = pl.BlockSpec(memory_space=pltpu.VMEM)
    hbm = pl.BlockSpec(memory_space=pltpu.HBM)
    mine = pl.pallas_call(
        slab_kernel,
        in_specs=[hbm] * 4,
        out_specs=vmem,
        out_shape=jax.ShapeDtypeStruct((n_narrow, row_sub, pairs), jnp.float32),
        scratch_shapes=[
            pltpu.VMEM((ROWS, bands), jnp.float32),
            pltpu.VMEM((ROWS, bands), jnp.float32),
            pltpu.VMEM((1, pairs), jnp.int32),
            pltpu.VMEM((1, pairs), jnp.int32),
            pltpu.SemaphoreType.DMA((4,)),
        ],
        compiler_params=params(16),
        name="slab_rows",
    )(*(in_hbm(x) for x in (val_orb, cond_orb, pair_val, pair_cond)))

    def exchange(x, bit):
        return lax.ppermute(x, "narrow", [(i, i ^ bit) for i in range(n_narrow)])

    across = n_narrow - 1

    def between_chips(x, step, stride):
        pairs_of = []
        for w in range(n_wide):
            place = w // stride % RADIX
            to = w + (step[place] - place) * stride
            pairs_of += [(w * n_narrow + n, to * n_narrow + (n ^ across)) for n in range(n_narrow)]
        return lax.ppermute(x, ("wide", "narrow"), pairs_of)

    def in_order(blocks, stride, steps):
        blocks = by_digit(blocks, lax.rem(lax.div(lax.axis_index("wide"), stride), RADIX), steps)
        groups = blocks[0].shape[0] // row_sub
        if groups == 1:
            return jnp.concatenate(blocks, axis=0)
        joined = jnp.stack([block.reshape(groups, row_sub, pairs) for block in blocks], axis=1)
        return joined.reshape(-1, pairs)

    strides = []
    while RADIX ** (len(strides) + 1) <= n_wide:
        strides.append(n_wide // RADIX ** (len(strides) + 1))
    start = across if len(strides) % 2 else 0
    narrow = lax.axis_index("narrow")
    sent, own_block = mine[start], mine[start ^ across]
    for n in range(1, n_narrow):
        got = exchange(mine, n)
        sent = jnp.where(narrow == n, got[n ^ start], sent)
        own_block = jnp.where(narrow == n, got[n ^ start ^ across], own_block)
    pair_val, pair_cond, sent = lax.optimization_barrier((pair_val, pair_cond, sent))
    v = pl.pallas_call(
        val_kernel,
        in_specs=[vmem] * 3,
        out_specs=vmem,
        out_shape=jax.ShapeDtypeStruct((rows + ROWS, pairs), jnp.float32),
        compiler_params=params(24),
        name="val_columns",
    )(val_orb, e_val[None, :], pair_val)
    own = pl.pallas_call(
        dens_kernel,
        in_specs=[vmem] * 4,
        out_specs=vmem,
        out_shape=jax.ShapeDtypeStruct((rows, pairs), jnp.float32),
        compiler_params=params(24),
        name="densities",
    )(cond_orb, e_cond[None, :], pair_cond, v)
    columns = [own] + [exchange(own, n) for n in range(1, n_narrow)]
    got = [sent]
    for i, stride in enumerate(strides):
        steps = ROUNDS[i % len(ROUNDS)]
        if i == 0:
            got = [own_block] + [between_chips(sent, step, stride) for step in steps]
            *got, own = lax.optimization_barrier((*got, own))
        else:
            sent = in_order(got, strides[i - 1], ROUNDS[(i - 1) % len(ROUNDS)])
            got = [between_chips(sent, step, stride) for step in steps]
            sent, got[0] = lax.optimization_barrier((sent, got[0]))
            got = [exchange(sent, across)] + got
    terms = pl.pallas_call(
        columns_kernel,
        in_specs=[vmem] * n_narrow,
        out_specs=[vmem] * 2,
        out_shape=[jax.ShapeDtypeStruct((pairs, n_narrow * rows), jnp.bfloat16)] * 2,
        compiler_params=params(16),
        name="columns",
    )(*columns)
    out = pl.pallas_call(
        functools.partial(product_kernel, strides[-1], ROUNDS[(len(strides) - 1) % len(ROUNDS)], row_sub),
        in_specs=[vmem] * (3 + len(got)),
        out_specs=vmem,
        out_shape=jax.ShapeDtypeStruct(chi_in.shape[::-1], jnp.float32),
        compiler_params=params(16),
        name="product",
    )(chi_in.T, *terms, *got)
    return out.T


def solution(mesh):
    placed = (
        P("wide", "narrow"),
        P(("wide", "narrow"), None),
        P(("wide", "narrow"), None),
        P(),
        P(),
        P(),
        P(),
    )
    return jax.shard_map(
        shards, mesh=mesh, in_specs=placed, out_specs=P("wide", "narrow"), check_vma=False
    )
```

```python
import functools

import jax
import jax.numpy as jnp
from jax import lax
from jax.experimental import pallas as pl
from jax.experimental.pallas import tpu as pltpu
from jax.sharding import PartitionSpec as P

SLAB_DEV = 8
ROWS = 8
RADIX = 4
ROUNDS = (
    ((2, 3, 1, 0), (3, 2, 0, 1), (1, 0, 3, 2)),
    ((3, 2, 1, 0), (1, 0, 3, 2), (2, 3, 0, 1)),
)
CHUNK = 256
PIECES = 4
MIB = 1 << 20


def params(mib):
    return pltpu.CompilerParams(vmem_limit_bytes=mib * MIB)


def split(x, terms):
    out = []
    for _ in range(terms - 1):
        out.append(x.astype(jnp.bfloat16))
        x = x - out[-1].astype(jnp.float32)
    return out + [x.astype(jnp.bfloat16)]


def one_hot(idx, chunk):
    place = lax.broadcasted_iota(jnp.int32, (chunk, idx.shape[1]), 0)
    return jnp.where(place == (idx & (chunk - 1)), 1.0, 0.0).astype(jnp.bfloat16)


def by_chunk(rows, chunk):
    return jnp.concatenate([rows[:, at : at + chunk] for at in range(0, rows.shape[1], chunk)], axis=0)


def own_chunk(every, idx, chunk, r):
    chunk_of = idx >> (chunk.bit_length() - 1)
    out = every[:r]
    for c in range(1, every.shape[0] // r):
        out = jnp.where(chunk_of == c, every[c * r : (c + 1) * r], out)
    return out


def pick_few(rows, hot, idx):
    terms = split(by_chunk(rows, CHUNK), 2)
    m = terms[0].shape[0]
    every = jnp.dot(jnp.concatenate(terms, axis=0), hot, preferred_element_type=jnp.float32)
    return own_chunk(every[:m] + every[m:], idx, CHUNK, rows.shape[0])


def pick_many(rows, idx):
    hot = one_hot(idx, 2 * CHUNK)
    terms = jnp.concatenate(split(by_chunk(rows, 2 * CHUNK), 2), axis=1)
    every = jnp.dot(terms, jnp.concatenate([hot, hot], axis=0), preferred_element_type=jnp.float32)
    return own_chunk(every, idx, 2 * CHUNK, rows.shape[0])


def slab_kernel(val_ref, cond_ref, pv_ref, pc_ref, out_ref, val, cond, pv, pc, sems):
    cuts = [pl.ds(at, val.shape[1] // PIECES) for at in range(0, val.shape[1], val.shape[1] // PIECES)]
    moves = [(pv_ref, pv), (pc_ref, pc)]
    for src, dst in ((val_ref, val), (cond_ref, cond)):
        moves += [(src.at[pl.ds(0, ROWS), cut], dst.at[:, cut]) for cut in cuts]
    copies = [pltpu.make_async_copy(src, dst, sems.at[i]) for i, (src, dst) in enumerate(moves)]
    for copy in copies:
        copy.start(priority=1)
    copies[0].wait()
    hot_v = one_hot(pv[...], CHUNK)
    copies[1].wait()
    hot_c = one_hot(pc[...], CHUNK)
    for copy in copies[2 : 2 + PIECES]:
        copy.wait()
    dens = pick_few(val[...], hot_v, pv[...])
    for copy in copies[2 + PIECES :]:
        copy.wait()
    dens = dens * pick_few(cond[...], hot_c, pc[...])
    sub = out_ref.shape[1]
    for n in range(out_ref.shape[0]):
        out_ref[n] = dens[n * sub : (n + 1) * sub]


def with_energy(orb_ref, e_ref):
    return jnp.concatenate([orb_ref[...], jnp.broadcast_to(e_ref[...], (ROWS, e_ref.shape[1]))], axis=0)


def val_kernel(val_ref, ev_ref, pv_ref, out_ref):
    out_ref[...] = pick_many(with_energy(val_ref, ev_ref), pv_ref[...])


def dens_kernel(cond_ref, ec_ref, pc_ref, v_ref, out_ref):
    r = out_ref.shape[0]
    c = pick_many(with_energy(cond_ref, ec_ref), pc_ref[...])
    weight = 1.0 / (c[r : r + 1] - v_ref[r : r + 1])
    out_ref[...] = v_ref[:r] * c[:r] * weight


def by_source(parts, me):
    step = 1
    while step < len(parts):
        odd = (me & step) != 0
        parts = [jnp.where(odd, parts[j ^ step], parts[j]) for j in range(len(parts))]
        step *= 2
    return parts


def columns_kernel(*refs):
    *cols_refs, hi_ref, lo_ref = refs
    cols = by_source([ref[...] for ref in cols_refs], lax.axis_index("narrow"))
    hi_ref[...], lo_ref[...] = split(jnp.concatenate(cols, axis=0).T, 2)


def by_digit(parts, place, steps):
    from_place = [[here] + [step.index(here) for step in steps] for here in range(RADIX)]
    out = []
    for source in range(RADIX):
        part = parts[from_place[0].index(source)]
        for here in range(1, RADIX):
            part = jnp.where(place == here, parts[from_place[here].index(source)], part)
        out.append(part)
    return out


def product_kernel(stride, steps, sub, chi_ref, hi_ref, lo_ref, *refs):
    *rows_refs, out_ref = refs
    s_hi, s_lo = split(jnp.concatenate([ref[...] for ref in rows_refs], axis=0), 2)
    m = s_hi.shape[0]
    by_hi = jnp.dot(jnp.concatenate([s_hi, s_lo], axis=0), hi_ref[...], preferred_element_type=jnp.float32)
    by_lo = jnp.dot(s_hi, lo_ref[...], preferred_element_type=jnp.float32)
    total = by_hi[:m] + (by_hi[m:] + by_lo)
    place, each = lax.rem(lax.div(lax.axis_index("wide"), stride), RADIX), m // len(rows_refs)
    parts = by_digit([total[at : at + each] for at in range(0, m, each)], place, steps)
    rows = [part[at : at + sub] for at in range(0, each, sub) for part in parts]
    out_ref[...] = chi_ref[...] + jnp.concatenate(rows, axis=0)


def in_hbm(x):
    return pltpu.with_memory_space_constraint(x, pltpu.HBM)


def shards(chi_in, val_orb, cond_orb, e_val, e_cond, pair_val, pair_cond):
    n_wide, n_narrow = lax.axis_size("wide"), lax.axis_size("narrow")
    row_sub = SLAB_DEV // n_narrow
    pairs, rows, bands = pair_val.shape[1], val_orb.shape[0], val_orb.shape[1]
    vmem = pl.BlockSpec(memory_space=pltpu.VMEM)
    hbm = pl.BlockSpec(memory_space=pltpu.HBM)
    mine = pl.pallas_call(
        slab_kernel,
        in_specs=[hbm] * 4,
        out_specs=vmem,
        out_shape=jax.ShapeDtypeStruct((n_narrow, row_sub, pairs), jnp.float32),
        scratch_shapes=[
            pltpu.VMEM((ROWS, bands), jnp.float32),
            pltpu.VMEM((ROWS, bands), jnp.float32),
            pltpu.VMEM((1, pairs), jnp.int32),
            pltpu.VMEM((1, pairs), jnp.int32),
            pltpu.SemaphoreType.DMA((2 + 2 * PIECES,)),
        ],
        compiler_params=params(16),
        name="slab_rows",
    )(*(in_hbm(x) for x in (val_orb, cond_orb, pair_val, pair_cond)))

    def exchange(x, bit):
        return lax.ppermute(x, "narrow", [(i, i ^ bit) for i in range(n_narrow)])

    across = n_narrow - 1

    def between_chips(x, step, stride):
        pairs_of = []
        for w in range(n_wide):
            place = w // stride % RADIX
            to = w + (step[place] - place) * stride
            pairs_of += [(w * n_narrow + n, to * n_narrow + (n ^ across)) for n in range(n_narrow)]
        return lax.ppermute(x, ("wide", "narrow"), pairs_of)

    def in_order(blocks, stride, steps):
        blocks = by_digit(blocks, lax.rem(lax.div(lax.axis_index("wide"), stride), RADIX), steps)
        groups = blocks[0].shape[0] // row_sub
        if groups == 1:
            return jnp.concatenate(blocks, axis=0)
        joined = jnp.stack([block.reshape(groups, row_sub, pairs) for block in blocks], axis=1)
        return joined.reshape(-1, pairs)

    strides = []
    while RADIX ** (len(strides) + 1) <= n_wide:
        strides.append(n_wide // RADIX ** (len(strides) + 1))
    start = across if len(strides) % 2 else 0
    narrow = lax.axis_index("narrow")
    sent, own_block = mine[start], mine[start ^ across]
    for n in range(1, n_narrow):
        got = exchange(mine, n)
        sent = jnp.where(narrow == n, got[n ^ start], sent)
        own_block = jnp.where(narrow == n, got[n ^ start ^ across], own_block)
    pair_val, pair_cond, sent = lax.optimization_barrier((pair_val, pair_cond, sent))
    v = pl.pallas_call(
        val_kernel,
        in_specs=[vmem] * 3,
        out_specs=vmem,
        out_shape=jax.ShapeDtypeStruct((rows + ROWS, pairs), jnp.float32),
        compiler_params=params(24),
        name="val_columns",
    )(val_orb, e_val[None, :], pair_val)
    own = pl.pallas_call(
        dens_kernel,
        in_specs=[vmem] * 4,
        out_specs=vmem,
        out_shape=jax.ShapeDtypeStruct((rows, pairs), jnp.float32),
        compiler_params=params(24),
        name="densities",
    )(cond_orb, e_cond[None, :], pair_cond, v)
    columns = [own] + [exchange(own, n) for n in range(1, n_narrow)]
    got = [sent]
    for i, stride in enumerate(strides):
        steps = ROUNDS[i % len(ROUNDS)]
        if i == 0:
            got = [own_block] + [between_chips(sent, step, stride) for step in steps]
            *got, own = lax.optimization_barrier((*got, own))
        else:
            sent = in_order(got, strides[i - 1], ROUNDS[(i - 1) % len(ROUNDS)])
            got = [between_chips(sent, step, stride) for step in steps]
            sent, got[0] = lax.optimization_barrier((sent, got[0]))
            got = [exchange(sent, across)] + got
    terms = pl.pallas_call(
        columns_kernel,
        in_specs=[vmem] * n_narrow,
        out_specs=[vmem] * 2,
        out_shape=[jax.ShapeDtypeStruct((pairs, n_narrow * rows), jnp.bfloat16)] * 2,
        compiler_params=params(16),
        name="columns",
    )(*columns)
    out = pl.pallas_call(
        functools.partial(product_kernel, strides[-1], ROUNDS[(len(strides) - 1) % len(ROUNDS)], row_sub),
        in_specs=[vmem] * (3 + len(got)),
        out_specs=vmem,
        out_shape=jax.ShapeDtypeStruct(chi_in.shape[::-1], jnp.float32),
        compiler_params=params(16),
        name="product",
    )(chi_in.T, *terms, *got)
    return out.T


def solution(mesh):
    placed = (
        P("wide", "narrow"),
        P(("wide", "narrow"), None),
        P(("wide", "narrow"), None),
        P(),
        P(),
        P(),
        P(),
    )
    return jax.shard_map(
        shards, mesh=mesh, in_specs=placed, out_specs=P("wide", "narrow"), check_vma=False
    )
```

```python
import functools

import jax
import jax.numpy as jnp
from jax import lax
from jax.experimental import pallas as pl
from jax.experimental.pallas import tpu as pltpu
from jax.sharding import PartitionSpec as P

SLAB_DEV = 8
ROWS = 8
RADIX = 4
ROUNDS = (
    ((2, 3, 1, 0), (3, 2, 0, 1), (1, 0, 3, 2)),
    ((3, 2, 1, 0), (1, 0, 3, 2), (2, 3, 0, 1)),
)
CHUNK = 256
PIECES = 4
MIB = 1 << 20


def params(mib):
    return pltpu.CompilerParams(vmem_limit_bytes=mib * MIB)


def split(x, terms):
    out = []
    for _ in range(terms - 1):
        out.append(x.astype(jnp.bfloat16))
        x = x - out[-1].astype(jnp.float32)
    return out + [x.astype(jnp.bfloat16)]


def one_hot(idx, chunk):
    place = lax.broadcasted_iota(jnp.int32, (chunk, idx.shape[1]), 0)
    return jnp.where(place == (idx & (chunk - 1)), 1.0, 0.0).astype(jnp.bfloat16)


def by_chunk(rows, chunk):
    return jnp.concatenate([rows[:, at : at + chunk] for at in range(0, rows.shape[1], chunk)], axis=0)


def own_chunk(every, idx, chunk, r):
    chunk_of = idx >> (chunk.bit_length() - 1)
    out = every[:r]
    for c in range(1, every.shape[0] // r):
        out = jnp.where(chunk_of == c, every[c * r : (c + 1) * r], out)
    return out


def pick_few(rows, hot, idx):
    terms = split(by_chunk(rows, CHUNK), 2)
    m = terms[0].shape[0]
    every = jnp.dot(jnp.concatenate(terms, axis=0), hot, preferred_element_type=jnp.float32)
    return own_chunk(every[:m] + every[m:], idx, CHUNK, rows.shape[0])


def pick_many(rows, idx):
    hot = one_hot(idx, 2 * CHUNK)
    terms = jnp.concatenate(split(by_chunk(rows, 2 * CHUNK), 2), axis=1)
    every = jnp.dot(terms, jnp.concatenate([hot, hot], axis=0), preferred_element_type=jnp.float32)
    return own_chunk(every, idx, 2 * CHUNK, rows.shape[0])


def slab_kernel(val_ref, cond_ref, pv_ref, pc_ref, out_ref, val, cond, pv, pc, sems):
    cuts = [pl.ds(at, val.shape[1] // PIECES) for at in range(0, val.shape[1], val.shape[1] // PIECES)]
    moves = [(pv_ref, pv), (pc_ref, pc)]
    for src, dst in ((val_ref, val), (cond_ref, cond)):
        moves += [(src.at[pl.ds(0, ROWS), cut], dst.at[:, cut]) for cut in cuts]
    copies = [pltpu.make_async_copy(src, dst, sems.at[i]) for i, (src, dst) in enumerate(moves)]
    for copy in copies:
        copy.start(priority=1)
    copies[0].wait()
    hot_v = one_hot(pv[...], CHUNK)
    copies[1].wait()
    hot_c = one_hot(pc[...], CHUNK)
    for copy in copies[2 : 2 + PIECES]:
        copy.wait()
    dens = pick_few(val[...], hot_v, pv[...])
    for copy in copies[2 + PIECES :]:
        copy.wait()
    dens = dens * pick_few(cond[...], hot_c, pc[...])
    sub = out_ref.shape[1]
    for n in range(out_ref.shape[0]):
        out_ref[n] = dens[n * sub : (n + 1) * sub]


def with_energy(orb_ref, e_ref):
    return jnp.concatenate([orb_ref[...], jnp.broadcast_to(e_ref[...], (ROWS, e_ref.shape[1]))], axis=0)


def val_kernel(val_ref, ev_ref, pv_ref, out_ref):
    out_ref[...] = pick_many(with_energy(val_ref, ev_ref), pv_ref[...])


def dens_kernel(cond_ref, ec_ref, pc_ref, v_ref, out_ref):
    r = out_ref.shape[0]
    c = pick_many(with_energy(cond_ref, ec_ref), pc_ref[...])
    weight = 1.0 / (c[r : r + 1] - v_ref[r : r + 1])
    out_ref[...] = v_ref[:r] * c[:r] * weight


def by_source(parts, me):
    step = 1
    while step < len(parts):
        odd = (me & step) != 0
        parts = [jnp.where(odd, parts[j ^ step], parts[j]) for j in range(len(parts))]
        step *= 2
    return parts


def columns_kernel(*refs):
    *cols_refs, hi_ref, lo_ref = refs
    cols = by_source([ref[...] for ref in cols_refs], lax.axis_index("narrow"))
    hi_ref[...], lo_ref[...] = split(jnp.concatenate(cols, axis=0).T, 2)


def by_digit(parts, place, steps):
    from_place = [[here] + [step.index(here) for step in steps] for here in range(RADIX)]
    out = []
    for source in range(RADIX):
        part = parts[from_place[0].index(source)]
        for here in range(1, RADIX):
            part = jnp.where(place == here, parts[from_place[here].index(source)], part)
        out.append(part)
    return out


def product_kernel(stride, steps, sub, chi_ref, hi_ref, lo_ref, *refs):
    *rows_refs, out_ref = refs
    s_hi, s_lo = split(jnp.concatenate([ref[...] for ref in rows_refs], axis=0), 2)
    m = s_hi.shape[0]
    by_hi = jnp.dot(jnp.concatenate([s_hi, s_lo], axis=0), hi_ref[...], preferred_element_type=jnp.float32)
    by_lo = jnp.dot(s_hi, lo_ref[...], preferred_element_type=jnp.float32)
    total = by_hi[:m] + (by_hi[m:] + by_lo)
    place, each = lax.rem(lax.div(lax.axis_index("wide"), stride), RADIX), m // len(rows_refs)
    parts = by_digit([total[at : at + each] for at in range(0, m, each)], place, steps)
    rows = [part[at : at + sub] for at in range(0, each, sub) for part in parts]
    out_ref[...] = chi_ref[...] + jnp.concatenate(rows, axis=0)


def in_hbm(x):
    return pltpu.with_memory_space_constraint(x, pltpu.HBM)


def shards(chi_in, val_orb, cond_orb, e_val, e_cond, pair_val, pair_cond):
    n_wide, n_narrow = lax.axis_size("wide"), lax.axis_size("narrow")
    row_sub = SLAB_DEV // n_narrow
    pairs, rows, bands = pair_val.shape[1], val_orb.shape[0], val_orb.shape[1]
    vmem = pl.BlockSpec(memory_space=pltpu.VMEM)
    hbm = pl.BlockSpec(memory_space=pltpu.HBM)
    mine = pl.pallas_call(
        slab_kernel,
        in_specs=[hbm] * 4,
        out_specs=vmem,
        out_shape=jax.ShapeDtypeStruct((n_narrow, row_sub, pairs), jnp.float32),
        scratch_shapes=[
            pltpu.VMEM((ROWS, bands), jnp.float32),
            pltpu.VMEM((ROWS, bands), jnp.float32),
            pltpu.VMEM((1, pairs), jnp.int32),
            pltpu.VMEM((1, pairs), jnp.int32),
            pltpu.SemaphoreType.DMA((2 + 2 * PIECES,)),
        ],
        compiler_params=params(16),
        name="slab_rows",
    )(*(in_hbm(x) for x in (val_orb, cond_orb, pair_val, pair_cond)))

    def exchange(x, bit):
        return lax.ppermute(x, "narrow", [(i, i ^ bit) for i in range(n_narrow)])

    across = n_narrow - 1

    def between_chips(x, step, stride):
        pairs_of = []
        for w in range(n_wide):
            place = w // stride % RADIX
            to = w + (step[place] - place) * stride
            pairs_of += [(w * n_narrow + n, to * n_narrow + (n ^ across)) for n in range(n_narrow)]
        return lax.ppermute(x, ("wide", "narrow"), pairs_of)

    def in_order(blocks, stride, steps):
        blocks = by_digit(blocks, lax.rem(lax.div(lax.axis_index("wide"), stride), RADIX), steps)
        groups = blocks[0].shape[0] // row_sub
        if groups == 1:
            return jnp.concatenate(blocks, axis=0)
        joined = jnp.stack([block.reshape(groups, row_sub, pairs) for block in blocks], axis=1)
        return joined.reshape(-1, pairs)

    strides = []
    while RADIX ** (len(strides) + 1) <= n_wide:
        strides.append(n_wide // RADIX ** (len(strides) + 1))
    start = across if len(strides) % 2 else 0
    narrow = lax.axis_index("narrow")
    pair_val, mine = lax.optimization_barrier((pair_val, mine))
    v = pl.pallas_call(
        val_kernel,
        in_specs=[vmem] * 3,
        out_specs=vmem,
        out_shape=jax.ShapeDtypeStruct((rows + ROWS, pairs), jnp.float32),
        compiler_params=params(24),
        name="val_columns",
    )(val_orb, e_val[None, :], pair_val)
    sent, own_block = mine[start], mine[start ^ across]
    for n in range(1, n_narrow):
        got, v = lax.optimization_barrier((exchange(mine, n), v))
        sent = jnp.where(narrow == n, got[n ^ start], sent)
        own_block = jnp.where(narrow == n, got[n ^ start ^ across], own_block)
    pair_cond, sent = lax.optimization_barrier((pair_cond, sent))
    own = pl.pallas_call(
        dens_kernel,
        in_specs=[vmem] * 4,
        out_specs=vmem,
        out_shape=jax.ShapeDtypeStruct((rows, pairs), jnp.float32),
        compiler_params=params(24),
        name="densities",
    )(cond_orb, e_cond[None, :], pair_cond, v)
    columns = [own] + [exchange(own, n) for n in range(1, n_narrow)]
    got = [sent]
    for i, stride in enumerate(strides):
        steps = ROUNDS[i % len(ROUNDS)]
        if i == 0:
            got = [own_block] + [between_chips(sent, step, stride) for step in steps]
            *got, own = lax.optimization_barrier((*got, own))
        else:
            sent = in_order(got, strides[i - 1], ROUNDS[(i - 1) % len(ROUNDS)])
            got = [between_chips(sent, step, stride) for step in steps]
            sent, got[0] = lax.optimization_barrier((sent, got[0]))
            got = [exchange(sent, across)] + got
    terms = pl.pallas_call(
        columns_kernel,
        in_specs=[vmem] * n_narrow,
        out_specs=[vmem] * 2,
        out_shape=[jax.ShapeDtypeStruct((pairs, n_narrow * rows), jnp.bfloat16)] * 2,
        compiler_params=params(16),
        name="columns",
    )(*columns)
    out = pl.pallas_call(
        functools.partial(product_kernel, strides[-1], ROUNDS[(len(strides) - 1) % len(ROUNDS)], row_sub),
        in_specs=[vmem] * (3 + len(got)),
        out_specs=vmem,
        out_shape=jax.ShapeDtypeStruct(chi_in.shape[::-1], jnp.float32),
        compiler_params=params(16),
        name="product",
    )(chi_in.T, *terms, *got)
    return out.T


def solution(mesh):
    placed = (
        P("wide", "narrow"),
        P(("wide", "narrow"), None),
        P(("wide", "narrow"), None),
        P(),
        P(),
        P(),
        P(),
    )
    return jax.shard_map(
        shards, mesh=mesh, in_specs=placed, out_specs=P("wide", "narrow"), check_vma=False
    )
```

```python
import functools

import jax
import jax.numpy as jnp
from jax import lax
from jax.experimental import pallas as pl
from jax.experimental.pallas import tpu as pltpu
from jax.sharding import PartitionSpec as P

SLAB_DEV = 8
ROWS = 8
RADIX = 4
ROUNDS = (
    ((2, 3, 1, 0), (3, 2, 0, 1), (1, 0, 3, 2)),
    ((3, 2, 1, 0), (2, 3, 0, 1), (1, 0, 3, 2)),
)
CHUNK = 256
PIECES = 4
MIB = 1 << 20


def params(mib):
    return pltpu.CompilerParams(vmem_limit_bytes=mib * MIB)


def split(x, terms):
    out = []
    for _ in range(terms - 1):
        out.append(x.astype(jnp.bfloat16))
        x = x - out[-1].astype(jnp.float32)
    return out + [x.astype(jnp.bfloat16)]


def one_hot(idx, chunk):
    place = lax.broadcasted_iota(jnp.int32, (chunk, idx.shape[1]), 0)
    return jnp.where(place == (idx & (chunk - 1)), 1.0, 0.0).astype(jnp.bfloat16)


def by_chunk(rows, chunk):
    return jnp.concatenate([rows[:, at : at + chunk] for at in range(0, rows.shape[1], chunk)], axis=0)


def own_chunk(every, idx, chunk, r):
    chunk_of = idx >> (chunk.bit_length() - 1)
    out = every[:r]
    for c in range(1, every.shape[0] // r):
        out = jnp.where(chunk_of == c, every[c * r : (c + 1) * r], out)
    return out


def pick_few(rows, hot, idx):
    terms = split(by_chunk(rows, CHUNK), 2)
    m = terms[0].shape[0]
    every = jnp.dot(jnp.concatenate(terms, axis=0), hot, preferred_element_type=jnp.float32)
    return own_chunk(every[:m] + every[m:], idx, CHUNK, rows.shape[0])


def pick_many(rows, idx):
    hot = one_hot(idx, 2 * CHUNK)
    terms = jnp.concatenate(split(by_chunk(rows, 2 * CHUNK), 2), axis=1)
    every = jnp.dot(terms, jnp.concatenate([hot, hot], axis=0), preferred_element_type=jnp.float32)
    return own_chunk(every, idx, 2 * CHUNK, rows.shape[0])


def slab_kernel(val_ref, cond_ref, pv_ref, pc_ref, out_ref, val, cond, pv, pc, sems):
    cuts = [pl.ds(at, val.shape[1] // PIECES) for at in range(0, val.shape[1], val.shape[1] // PIECES)]
    moves = [(pv_ref, pv), (pc_ref, pc)]
    for src, dst in ((val_ref, val), (cond_ref, cond)):
        moves += [(src.at[pl.ds(0, ROWS), cut], dst.at[:, cut]) for cut in cuts]
    copies = [pltpu.make_async_copy(src, dst, sems.at[i]) for i, (src, dst) in enumerate(moves)]
    for copy in copies:
        copy.start(priority=1)
    copies[0].wait()
    hot_v = one_hot(pv[...], CHUNK)
    copies[1].wait()
    hot_c = one_hot(pc[...], CHUNK)
    for copy in copies[2 : 2 + PIECES]:
        copy.wait()
    dens = pick_few(val[...], hot_v, pv[...])
    for copy in copies[2 + PIECES :]:
        copy.wait()
    dens = dens * pick_few(cond[...], hot_c, pc[...])
    sub = out_ref.shape[1]
    for n in range(out_ref.shape[0]):
        out_ref[n] = dens[n * sub : (n + 1) * sub]


def with_energy(orb_ref, e_ref):
    return jnp.concatenate([orb_ref[...], jnp.broadcast_to(e_ref[...], (ROWS, e_ref.shape[1]))], axis=0)


def val_kernel(val_ref, ev_ref, pv_ref, out_ref):
    out_ref[...] = pick_many(with_energy(val_ref, ev_ref), pv_ref[...])


def dens_kernel(cond_ref, ec_ref, pc_ref, v_ref, out_ref):
    r = out_ref.shape[0]
    c = pick_many(with_energy(cond_ref, ec_ref), pc_ref[...])
    weight = 1.0 / (c[r : r + 1] - v_ref[r : r + 1])
    out_ref[...] = v_ref[:r] * c[:r] * weight


def by_source(parts, me):
    step = 1
    while step < len(parts):
        odd = (me & step) != 0
        parts = [jnp.where(odd, parts[j ^ step], parts[j]) for j in range(len(parts))]
        step *= 2
    return parts


def columns_kernel(*refs):
    *cols_refs, hi_ref, lo_ref = refs
    cols = by_source([ref[...] for ref in cols_refs], lax.axis_index("narrow"))
    hi_ref[...], lo_ref[...] = split(jnp.concatenate(cols, axis=0).T, 2)


def by_digit(parts, place, steps):
    from_place = [[here] + [step.index(here) for step in steps] for here in range(RADIX)]
    out = []
    for source in range(RADIX):
        part = parts[from_place[0].index(source)]
        for here in range(1, RADIX):
            part = jnp.where(place == here, parts[from_place[here].index(source)], part)
        out.append(part)
    return out


def product_kernel(stride, steps, sub, chi_ref, hi_ref, lo_ref, *refs):
    *rows_refs, out_ref = refs
    s_hi, s_lo = split(jnp.concatenate([ref[...] for ref in rows_refs], axis=0), 2)
    m = s_hi.shape[0]
    by_hi = jnp.dot(jnp.concatenate([s_hi, s_lo], axis=0), hi_ref[...], preferred_element_type=jnp.float32)
    by_lo = jnp.dot(s_hi, lo_ref[...], preferred_element_type=jnp.float32)
    total = by_hi[:m] + (by_hi[m:] + by_lo)
    place, each = lax.rem(lax.div(lax.axis_index("wide"), stride), RADIX), m // len(rows_refs)
    parts = by_digit([total[at : at + each] for at in range(0, m, each)], place, steps)
    rows = [part[at : at + sub] for at in range(0, each, sub) for part in parts]
    out_ref[...] = chi_ref[...] + jnp.concatenate(rows, axis=0)


def in_hbm(x):
    return pltpu.with_memory_space_constraint(x, pltpu.HBM)


def shards(chi_in, val_orb, cond_orb, e_val, e_cond, pair_val, pair_cond):
    n_wide, n_narrow = lax.axis_size("wide"), lax.axis_size("narrow")
    row_sub = SLAB_DEV // n_narrow
    pairs, rows, bands = pair_val.shape[1], val_orb.shape[0], val_orb.shape[1]
    vmem = pl.BlockSpec(memory_space=pltpu.VMEM)
    hbm = pl.BlockSpec(memory_space=pltpu.HBM)
    mine = pl.pallas_call(
        slab_kernel,
        in_specs=[hbm] * 4,
        out_specs=vmem,
        out_shape=jax.ShapeDtypeStruct((n_narrow, row_sub, pairs), jnp.float32),
        scratch_shapes=[
            pltpu.VMEM((ROWS, bands), jnp.float32),
            pltpu.VMEM((ROWS, bands), jnp.float32),
            pltpu.VMEM((1, pairs), jnp.int32),
            pltpu.VMEM((1, pairs), jnp.int32),
            pltpu.SemaphoreType.DMA((2 + 2 * PIECES,)),
        ],
        compiler_params=params(16),
        name="slab_rows",
    )(*(in_hbm(x) for x in (val_orb, cond_orb, pair_val, pair_cond)))

    def exchange(x, bit):
        return lax.ppermute(x, "narrow", [(i, i ^ bit) for i in range(n_narrow)])

    across = n_narrow - 1

    def between_chips(x, step, stride):
        pairs_of = []
        for w in range(n_wide):
            place = w // stride % RADIX
            to = w + (step[place] - place) * stride
            pairs_of += [(w * n_narrow + n, to * n_narrow + (n ^ across)) for n in range(n_narrow)]
        return lax.ppermute(x, ("wide", "narrow"), pairs_of)

    def in_order(blocks, stride, steps):
        blocks = by_digit(blocks, lax.rem(lax.div(lax.axis_index("wide"), stride), RADIX), steps)
        groups = blocks[0].shape[0] // row_sub
        if groups == 1:
            return jnp.concatenate(blocks, axis=0)
        joined = jnp.stack([block.reshape(groups, row_sub, pairs) for block in blocks], axis=1)
        return joined.reshape(-1, pairs)

    strides = []
    while RADIX ** (len(strides) + 1) <= n_wide:
        strides.append(n_wide // RADIX ** (len(strides) + 1))
    start = across if len(strides) % 2 else 0
    narrow = lax.axis_index("narrow")
    sent, own_block = mine[start], mine[start ^ across]
    for n in range(1, n_narrow):
        got = exchange(mine, n)
        sent = jnp.where(narrow == n, got[n ^ start], sent)
        own_block = jnp.where(narrow == n, got[n ^ start ^ across], own_block)
    pair_val, pair_cond, sent = lax.optimization_barrier((pair_val, pair_cond, sent))
    v = pl.pallas_call(
        val_kernel,
        in_specs=[vmem] * 3,
        out_specs=vmem,
        out_shape=jax.ShapeDtypeStruct((rows + ROWS, pairs), jnp.float32),
        compiler_params=params(24),
        name="val_columns",
    )(val_orb, e_val[None, :], pair_val)
    own = pl.pallas_call(
        dens_kernel,
        in_specs=[vmem] * 4,
        out_specs=vmem,
        out_shape=jax.ShapeDtypeStruct((rows, pairs), jnp.float32),
        compiler_params=params(24),
        name="densities",
    )(cond_orb, e_cond[None, :], pair_cond, v)
    columns = [own] + [exchange(own, n) for n in range(1, n_narrow)]
    got = [sent]
    for i, stride in enumerate(strides):
        steps = ROUNDS[i % len(ROUNDS)]
        if i == 0:
            got = [own_block] + [between_chips(sent, step, stride) for step in steps]
            *got, own = lax.optimization_barrier((*got, own))
        else:
            sent = in_order(got, strides[i - 1], ROUNDS[(i - 1) % len(ROUNDS)])
            got = [between_chips(sent, step, stride) for step in steps]
            sent, got[0] = lax.optimization_barrier((sent, got[0]))
            got = [exchange(sent, across)] + got
    terms = pl.pallas_call(
        columns_kernel,
        in_specs=[vmem] * n_narrow,
        out_specs=[vmem] * 2,
        out_shape=[jax.ShapeDtypeStruct((pairs, n_narrow * rows), jnp.bfloat16)] * 2,
        compiler_params=params(16),
        name="columns",
    )(*columns)
    out = pl.pallas_call(
        functools.partial(product_kernel, strides[-1], ROUNDS[(len(strides) - 1) % len(ROUNDS)], row_sub),
        in_specs=[vmem] * (3 + len(got)),
        out_specs=vmem,
        out_shape=jax.ShapeDtypeStruct(chi_in.shape[::-1], jnp.float32),
        compiler_params=params(16),
        name="product",
    )(chi_in.T, *terms, *got)
    return out.T


def solution(mesh):
    placed = (
        P("wide", "narrow"),
        P(("wide", "narrow"), None),
        P(("wide", "narrow"), None),
        P(),
        P(),
        P(),
        P(),
    )
    return jax.shard_map(
        shards, mesh=mesh, in_specs=placed, out_specs=P("wide", "narrow"), check_vma=False
    )
```
